512 devices in a mesh: band: 64 (over z, x, core), lon: 8 (over y).
Axes of the slice: x: 4, y: 8, z: 8, core: 2. Of those that a mesh axis runs over, the one named last changes fastest.
Arguments:
- spectral_in: float32 [512, 32, 641], P(('band', 'lon')), may hold values from -6 to 6
- leg_synthesis: float32 [512, 641, 640], P(('band', 'lon')), may hold values from -0.25 to 0.25
- leg_analysis: float32 [512, 640, 641], P(('band', 'lon')), may hold values from -0.15625 to 0.15625
- slot_pair: int32 [512], replicated, may hold values from 0 to 320, as said below
- departure_cells: int32 [1280, 2560], P('band'), may hold values from 0 to 3
- departure_frac: float32 [1280, 2560], P('band'), may hold values from 0 to 1
Outputs:
- spectral_out: float32 [512, 32, 641], P(('band', 'lon'))
The draws below stay inside these ranges and needn't reach their ends.
Inputs may be any that keep to these rules, and one draw needn't show every extreme that they name: `slot_pair`: every pair 0 to 319 stands in exactly one slot; the value 320 marks an empty slot; all slots of at least one index of band hold pairs.
All inputs are finite; a program needn't handle non-finite values.
Results may differ from the reference program's by a relative error of at most 0.0003.
Values sent between devices are 32-bit elements; how exact they have to be, the bound alone decides.
No kernel may reach another device: no remote copies, remote signals or barrier semaphores. Data moves between devices by JAX's collectives and lax.ppermute only.
A program may use at most 64 MiB of HBM per device.

```python
import jax
import jax.numpy as jnp
from jax import lax

WAVES = 640
PAIRS = 320
ROWS = 641
NLAT = 1280
NLON = 2560
VARS = 16
SLOT_DEV = 1
SLOTS = 512
REACH = 4
N_BAND = 64
N_LON = 8


def draw_slot_pair(key, part):
    key = jax.random.fold_in(key, 7)
    owner_key, order_key, pair_key = jax.random.split(key, 3)
    slot_index = jnp.arange(SLOTS, dtype=jnp.int32)
    owner_band = slot_index // (N_LON * SLOT_DEV)
    filled_band = jax.random.randint(owner_key, (), 0, N_BAND)
    scores = jax.random.permutation(order_key, SLOTS).astype(jnp.int32) + jnp.where(owner_band == filled_band, SLOTS, 0).astype(jnp.int32)
    ranking = jnp.argsort(-scores)
    slot_rank = jnp.zeros(SLOTS, jnp.int32).at[ranking].set(slot_index)
    pair_order = jax.random.permutation(pair_key, PAIRS).astype(jnp.int32)
    chosen_pair = jnp.take(pair_order, jnp.minimum(slot_rank, PAIRS - 1))
    return jnp.where(slot_rank < PAIRS, chosen_pair, PAIRS).astype(jnp.int32)


def plant(result, key, least, top_value):
    longest = result.shape.index(max(result.shape))
    spots = []
    for shift in (0, 1):
        where = [jax.random.randint(jax.random.fold_in(key, axis), (), 0, length) for axis, length in enumerate(result.shape)]
        where[longest] = (where[longest] + shift) % result.shape[longest]
        spots.append(tuple(where))
    return result.at[spots[0]].set(least).at[spots[1]].set(top_value)


def steps_of(rng, extent, pieces, low, top_value):
    def one(dim, shards_of):
        heights = jax.random.uniform(jax.random.fold_in(jax.random.fold_in(rng, 6), dim), (shards_of,), jnp.float32, low / len(pieces), top_value / len(pieces))
        return jnp.repeat(jnp.exp(heights), extent[dim] // shards_of).reshape((-1,) + (1,) * (len(extent) - dim - 1))

    level = one(*pieces[0])
    for cut in pieces[1:]:
        level = level * one(*cut)
    return level


def gaussian(own_key, shape, deviation, reach, cuts=(), held_as=jnp.bfloat16):
    values = deviation * jax.random.normal(own_key, shape, jnp.float32)
    if cuts:
        values = values * steps_of(own_key, shape, cuts, -0.22, 0.18)
    return jnp.clip(values, -reach, reach).astype(held_as)


def setup_inputs(seed: int = 0) -> dict:
    streams_of = jax.random.split(jax.random.key(seed), 7)
    spectral_in = gaussian(streams_of[0], (SLOTS, 2 * VARS, ROWS), 1.0, 6.0, ((0, 512),), jnp.float32)
    leg_synthesis = gaussian(streams_of[1], (SLOTS, ROWS, NLAT // 2), ROWS ** -0.5, 0.25, ((0, 512),), jnp.float32)
    leg_analysis = gaussian(streams_of[2], (SLOTS, NLAT // 2, ROWS), NLAT ** -0.5, 0.15625, ((0, 512),), jnp.float32)
    slot_pair = draw_slot_pair(jax.random.fold_in(streams_of[6], 71), 0)
    departure_cells = plant(jax.random.randint(streams_of[4], (NLAT, NLON), 0, REACH), jax.random.fold_in(streams_of[4], 1), 0, REACH - 1).astype(jnp.int32)
    departure_frac = jnp.clip(1.0 * jax.random.uniform(streams_of[5], (NLAT, NLON), jnp.float32) ** steps_of(streams_of[5], (NLAT, NLON), ((0, 64),), -0.2, 0.2), 0.0, 1.0)
    return dict(spectral_in=spectral_in, leg_synthesis=leg_synthesis, leg_analysis=leg_analysis, slot_pair=slot_pair, departure_cells=departure_cells, departure_frac=departure_frac)


def row_masks(pair_ids):
    row_index = jnp.arange(ROWS, dtype=jnp.int32)[None, :]
    split_row = (WAVES - pair_ids)[:, None]
    upper_part = row_index < split_row
    parity = jnp.where(upper_part, row_index, row_index - split_row) % 2
    even_rows = (parity == 0).astype(jnp.float32)
    active = (pair_ids < PAIRS)[:, None]
    first_wave = jnp.logical_and(upper_part, active).astype(jnp.float32)
    second_wave = jnp.logical_and(jnp.logical_not(upper_part), active).astype(jnp.float32)
    return first_wave, second_wave, even_rows


def inverse_legendre(spectrum, table, pair_ids):
    first_wave, second_wave, even_rows = row_masks(pair_ids)
    row_signs = 2.0 * even_rows - 1.0
    weights = jnp.stack([first_wave, first_wave * row_signs, second_wave, second_wave * row_signs], axis=1)
    masked = spectrum[:, None, :, :] * weights[:, :, None, :]
    product = jnp.einsum("sacr,srh->sach", masked, table, precision=lax.Precision.HIGHEST)
    northern = product[:, 0::2]
    southern = product[:, 1::2]
    return jnp.concatenate([northern, jnp.flip(southern, axis=3)], axis=3)


def direct_legendre(fourier, table, pair_ids):
    half_lat = fourier.shape[3] // 2
    northern = fourier[..., :half_lat]
    southern = jnp.flip(fourier[..., half_lat:], axis=3)
    stacked = jnp.stack([northern + southern, northern - southern], axis=2)
    stacked = stacked.reshape(fourier.shape[0], 4, fourier.shape[2], half_lat)
    product = jnp.einsum("sach,shr->sacr", stacked, table, precision=lax.Precision.HIGHEST)
    first_wave, second_wave, even_rows = row_masks(pair_ids)
    odd_rows = 1.0 - even_rows
    weights = jnp.stack([first_wave * even_rows, first_wave * odd_rows, second_wave * even_rows, second_wave * odd_rows], axis=1)
    return jnp.sum(product * weights[:, :, None, :], axis=1)


def reference(spectral_in, leg_synthesis, leg_analysis, slot_pair, departure_cells, departure_frac):
    def inverse_one(operands):
        spectrum, synth_table, pair_id = operands
        return inverse_legendre(spectrum[None], synth_table[None], pair_id[None])[0]

    per_slot = lax.map(inverse_one, (spectral_in, leg_synthesis, slot_pair))
    seats = jnp.zeros(PAIRS + 1, jnp.int32).at[slot_pair].set(jnp.arange(SLOTS, dtype=jnp.int32))[:PAIRS]
    natural = jnp.concatenate([per_slot[seats, 0], per_slot[jnp.flip(seats), 1]], axis=0)
    spectrum = lax.complex(natural[:, :VARS], natural[:, VARS:])
    spectrum = jnp.transpose(spectrum, (2, 1, 0))
    spectrum = jnp.pad(spectrum, ((0, 0), (0, 0), (0, NLON // 2 + 1 - WAVES)))
    grid_field = jnp.fft.irfft(spectrum, n=NLON, axis=2) * NLON
    longitude = jnp.arange(NLON, dtype=jnp.int32)[None, None, :]
    shift_cells = departure_cells[:, None, :]
    fraction = departure_frac[:, None, :]
    near_index = jnp.broadcast_to((longitude - shift_cells) % NLON, grid_field.shape)
    far_index = jnp.broadcast_to((longitude - shift_cells - 1) % NLON, grid_field.shape)
    advected = (1.0 - fraction) * jnp.take_along_axis(grid_field, near_index, axis=2) + fraction * jnp.take_along_axis(grid_field, far_index, axis=2)
    transform = jnp.fft.rfft(advected, axis=2)[:, :, :WAVES] / NLON
    analysis = jnp.concatenate([jnp.real(transform), jnp.imag(transform)], axis=1)
    analysis = jnp.transpose(analysis, (2, 1, 0))

    def direct_one(operands):
        anal_table, pair_id = operands
        safe_pair = jnp.minimum(pair_id, PAIRS - 1)
        both_waves = jnp.stack([analysis[safe_pair], analysis[WAVES - 1 - safe_pair]])
        return direct_legendre(both_waves[None], anal_table[None], pair_id[None])[0]

    return lax.map(direct_one, (leg_analysis, slot_pair))
```

```python
import math

import jax
import jax.numpy as jnp
import ml_dtypes
import numpy as np
from jax import lax
from jax.experimental import pallas as pl
from jax.experimental.pallas import tpu as pltpu
from jax.sharding import PartitionSpec as P

WAVES = 640
PAIRS = 320
ROWS = 641
HALF = 640
NLON = 2560
SLOTS = 512
RADIX = 8
FINE = 80
SEG = 320
WIDE = 384
HALF_ROWS = 5
REACH = 4
BF = jnp.bfloat16
F32 = jnp.float32


def halves(table):
    high = table.astype(np.float32).astype(ml_dtypes.bfloat16)
    low = (table - high.astype(np.float64)).astype(np.float32).astype(ml_dtypes.bfloat16)
    return high, low


def fine_tables():
    place = np.arange(WIDE)
    place = np.where(place < SEG, place, place - WIDE)
    phase = (np.arange(FINE)[:, None] * place[None, :]) % SEG
    cos, sin = np.cos(2 * math.pi * phase / SEG), np.sin(2 * math.pi * phase / SEG)
    synth = np.zeros((256, 2 * WIDE))
    synth[0:FINE, :WIDE] = 2 * cos
    synth[0:FINE, WIDE:] = 2 * sin
    synth[128 : 128 + FINE, :WIDE] = -2 * sin
    synth[128 : 128 + FINE, WIDE:] = 2 * cos
    anal = np.zeros((2 * WIDE, 256))
    anal[:WIDE, 0:FINE] = cos.T / NLON
    anal[WIDE:, 0:FINE] = sin.T / NLON
    anal[:WIDE, 128 : 128 + FINE] = -sin.T / NLON
    anal[WIDE:, 128 : 128 + FINE] = cos.T / NLON
    turn = 2 * math.pi * ((np.arange(RADIX)[:, None] * place[None, :]) % NLON) / NLON
    twiddle = np.concatenate([np.cos(turn), np.sin(turn)], axis=0).astype(np.float32)
    return halves(synth), halves(anal), twiddle


def split(value):
    high = value.astype(BF)
    return high, (value - high.astype(F32)).astype(BF)


def dot3(left, right_high, right_low):
    high, low = split(left)
    rows = left.shape[0]
    both = jnp.dot(
        jnp.concatenate([high, low], axis=0), right_high, preferred_element_type=F32
    )
    return both[:rows] + both[rows:] + jnp.dot(high, right_low, preferred_element_type=F32)


def wave_rows(pair):
    row = lax.broadcasted_iota(jnp.int32, (1, ROWS), 1)
    cut = WAVES - pair
    upper = row < cut
    odd = jnp.where(upper, row, row - cut) & 1
    return upper, odd


def synthesis_kernel(slot_ref, pairs_ref, spec_ref, table_ref, out_ref, turned, staged):
    pair = pairs_ref[slot_ref[0]]
    upper, odd = wave_rows(pair)
    live = pair < PAIRS
    groups = []
    for parity in range(2):
        for half in range(2):
            for wave in range(2):
                mask = jnp.logical_and(upper if wave == 0 else jnp.logical_not(upper), odd == parity)
                mask = jnp.logical_and(mask, live)
                for part in range(2):
                    first = part * 16 + half * 8
                    groups.append(jnp.where(mask, spec_ref[0, first : first + 8, :], 0.0))
    table_high, table_low = split(table_ref[0])
    product = dot3(jnp.concatenate(groups, axis=0), table_high, table_low)
    even, odd_sum = product[:64], product[64:]
    turned[...] = jnp.concatenate([even + odd_sum, even - odd_sum], axis=0).T
    lane = lax.broadcasted_iota(jnp.int32, (128, 128), 1)
    left = lane < 64
    pick = [turned[pl.ds(u, 128, stride=5), :] for u in range(5)]
    rolled = [pltpu.roll(q, 64, 1) for q in pick]
    staged[pl.ds(0, 128, stride=2), :] = jnp.where(left, pick[0], rolled[1])
    staged[pl.ds(1, 128, stride=2), :] = jnp.where(left, pick[3], rolled[4])
    staged[pl.ds(256, 128, stride=2), :] = pick[2]
    staged[pl.ds(257, 128, stride=2), :] = pltpu.roll(pick[2], 96, 1)
    staged[pl.ds(512, 128, stride=2), :] = jnp.where(left, rolled[0], pick[1])
    staged[pl.ds(513, 128, stride=2), :] = jnp.where(left, rolled[3], pick[4])
    staged[pl.ds(768, 128, stride=2), :] = rolled[2]
    staged[pl.ds(769, 128, stride=2), :] = pltpu.roll(pick[2], 32, 1)
    out_ref[0:256, 0:128] = staged[0:256, :]
    out_ref[0:256, 128:256] = staged[256:512, :]
    for block in range(32):
        at = (63 - block) * 8
        out_ref[at : at + 8, 0:128] = staged[512 + block * 8 : 512 + block * 8 + 8, :]
        out_ref[at : at + 8, 128:256] = staged[768 + block * 8 : 768 + block * 8 + 8, :]


def grid_kernel(
    in_ref, choice_ref, weight_ref, synth_h, synth_l, anal_h, anal_l, twiddle_ref, out_ref,
    coeff, spread, fields, back
):
    columns = in_ref[...].T[:160]
    high, low = split(columns)
    picked = jnp.dot(
        jnp.concatenate([high, low], axis=0), choice_ref[...], preferred_element_type=F32
    )
    lane = lax.broadcasted_iota(jnp.int32, (8, 128), 1)
    first_wave = lane < FINE // 2
    mean_scale = jnp.where(lane == 0, 0.5, 1.0)
    for level in range(2):
        for i in range(HALF_ROWS):
            for r in range(RADIX):
                for part in range(2):
                    base = level * 160 + i * 32 + part * 8
                    value = jnp.where(
                        first_wave,
                        picked[base : base + 8, r * 128 : r * 128 + 128],
                        picked[base + 16 : base + 24, r * 128 : r * 128 + 128],
                    )
                    if r == 0:
                        value = value * mean_scale
                    at = level * 320 + i * 64 + r * 8
                    coeff[at : at + 8, part * 128 : part * 128 + 128] = value
    both = coeff[...].astype(BF)
    wide = jnp.dot(both, synth_h[...], preferred_element_type=F32)
    spread[...] = (
        wide[:320] + wide[320:] + jnp.dot(both[:320], synth_l[...], preferred_element_type=F32)
    )
    root = math.sqrt(0.5)
    for i in range(HALF_ROWS):
        real, imag = [], []
        for r in range(RADIX):
            at = i * 64 + r * 8
            zr, zi = spread[at : at + 8, :WIDE], spread[at : at + 8, WIDE:]
            if r == 0:
                real.append(zr)
                imag.append(None)
                continue
            tr, ti = twiddle_ref[r : r + 1, :], twiddle_ref[RADIX + r : RADIX + r + 1, :]
            real.append(tr * zr - ti * zi)
            imag.append(None if r == 4 else tr * zi + ti * zr)
        plus, minus = real[0] + real[4], real[0] - real[4]
        p, n = real[2] + real[6], imag[2] - imag[6]
        evens = [plus + p, minus - n, plus - p, minus + n]
        a, b = real[1] + real[7], real[3] + real[5]
        c, d = imag[1] - imag[7], imag[3] - imag[5]
        odds = [a + b, root * ((a - b) - (c + d)), d - c, -root * ((a - b) + (c + d))]
        moved = []
        for k in range(RADIX):
            value = evens[k] + odds[k] if k < 4 else evens[k - 4] - odds[k - 4]
            total = weight_ref[i, k, 0:1, :] * value
            for offset in range(1, REACH + 1):
                total = total + weight_ref[i, k, offset : offset + 1, :] * pltpu.roll(
                    value, offset, 1
                )
            moved.append(total)
        s = [moved[k] + moved[k + 4] for k in range(4)]
        d = [moved[k] - moved[k + 4] for k in range(4)]
        s02, s13 = s[0] + s[2], s[1] + s[3]
        dd, ds = root * (d[1] - d[3]), root * (d[1] + d[3])
        waves = [
            (s02 + s13, None),
            (d[0] + dd, -d[2] - ds),
            (s[0] - s[2], s[3] - s[1]),
            (d[0] - dd, d[2] - ds),
            (s02 - s13, None),
        ]
        for r in range(RADIX):
            vr, vi = waves[r] if r < 5 else waves[8 - r]
            if r > 4:
                vi = -vi
            at = i * 64 + r * 8
            if r == 0:
                fields[at : at + 8, :WIDE] = vr
                fields[at : at + 8, WIDE:] = jnp.zeros_like(vr)
                continue
            tr, ti = twiddle_ref[r : r + 1, :], twiddle_ref[RADIX + r : RADIX + r + 1, :]
            if vi is None:
                fields[at : at + 8, :WIDE] = tr * vr
                fields[at : at + 8, WIDE:] = -ti * vr
            else:
                fields[at : at + 8, :WIDE] = tr * vr + ti * vi
                fields[at : at + 8, WIDE:] = tr * vi - ti * vr
    result = dot3(fields[...], anal_h[...], anal_l[...])
    for i in range(HALF_ROWS):
        for r in range(RADIX):
            for part in range(2):
                at = i * 64 + r * 8
                value = result[at : at + 8, part * 128 : part * 128 + 128]
                base = i * 32 + part * 8
                back[base : base + 8, r * 128 : r * 128 + 128] = jnp.where(first_wave, value, 0.0)
                back[base + 16 : base + 24, r * 128 : r * 128 + 128] = jnp.where(
                    first_wave, 0.0, value
                )
    high, low = split(back[...])
    across = (((1,), (1,)), ((), ()))
    choice = choice_ref[...]
    out_ref[:, 0:160] = lax.dot_general(
        choice, high, across, preferred_element_type=F32
    ) + lax.dot_general(choice, low, across, preferred_element_type=F32)
    out_ref[:, 160:256] = jnp.zeros((SLOTS, 96), F32)


def analysis_kernel(slot_ref, pairs_ref, in_ref, table_ref, out_ref, turned, staged):
    staged[0:256, :] = in_ref[0:256, 0:128]
    staged[256:512, :] = in_ref[0:256, 128:256]
    for block in range(32):
        at = (63 - block) * 8
        staged[512 + block * 8 : 512 + block * 8 + 8, :] = in_ref[at : at + 8, 0:128]
        staged[768 + block * 8 : 768 + block * 8 + 8, :] = in_ref[at : at + 8, 128:256]
    lane = lax.broadcasted_iota(jnp.int32, (128, 128), 1)
    left = lane < 64
    north_a, north_b, south_a, south_b = (
        [staged[pl.ds(256 * q + f, 128, stride=2), :] for f in range(2)] for q in range(4)
    )
    for f in range(2):
        turned[pl.ds(3 * f, 128, stride=5), :] = jnp.where(
            left, north_a[f], pltpu.roll(south_a[f], 64, 1)
        )
        turned[pl.ds(3 * f + 1, 128, stride=5), :] = jnp.where(
            left, pltpu.roll(north_a[f], 64, 1), south_a[f]
        )
    turned[pl.ds(2, 128, stride=5), :] = jnp.where(
        left,
        jnp.where(lane < 32, north_b[0], pltpu.roll(north_b[1], 32, 1)),
        jnp.where(lane < 96, pltpu.roll(south_b[0], 64, 1), pltpu.roll(south_b[1], 96, 1)),
    )
    straight = turned[...].T
    north, south_rows = straight[:64], straight[64:]
    table_high, table_low = split(table_ref[0])
    product = dot3(
        jnp.concatenate([north + south_rows, north - south_rows], axis=0), table_high, table_low
    )
    pair = pairs_ref[slot_ref[0]]
    upper, odd = wave_rows(pair)
    live = pair < PAIRS
    even = odd == 0
    for half in range(2):
        for part in range(2):
            rows = [
                [
                    product[
                        parity * 64 + half * 32 + wave * 16 + part * 8 :
                        parity * 64 + half * 32 + wave * 16 + part * 8 + 8
                    ]
                    for parity in range(2)
                ]
                for wave in range(2)
            ]
            value = jnp.where(
                upper,
                jnp.where(even, rows[0][0], rows[0][1]),
                jnp.where(even, rows[1][0], rows[1][1]),
            )
            first = part * 16 + half * 8
            out_ref[0, first : first + 8, :] = jnp.where(live, value, 0.0)


SMEM = pl.BlockSpec(memory_space=pltpu.SMEM)
VMEM = pl.BlockSpec(memory_space=pltpu.VMEM)
PARAMS = pltpu.CompilerParams(vmem_limit_bytes=40 * 1024 * 1024)


def legendre_scratch():
    return [pltpu.VMEM((HALF, 128), F32), pltpu.VMEM((1024, 128), F32)]


def slot_choice(slot_pair):
    block = jnp.arange(RADIX * 128, dtype=jnp.int32)
    fine, rest = block % 128, block // 128
    wave = fine * RADIX + rest
    pair = jnp.where(wave < PAIRS, wave, WAVES - 1 - wave)
    pair = jnp.where(fine < FINE, pair, -1)
    return (slot_pair[:, None] == pair[None, :]).astype(BF)


def advection_weights(cells, fraction, band, lon, bands):
    position = jnp.arange(HALF_ROWS, dtype=jnp.int32)
    position = jnp.where(lon % 2 == 0, position, (position + 1) % HALF_ROWS)
    row = (HALF_ROWS * lon + position) // 2
    row = jnp.where(band < bands // 2, row, cells.shape[0] - 1 - row)
    cells = jnp.take(cells, row, axis=0).reshape(HALF_ROWS, RADIX, 1, SEG)
    fraction = jnp.take(fraction, row, axis=0).reshape(HALF_ROWS, RADIX, 1, SEG)
    offset = jnp.arange(REACH + 1, dtype=jnp.int32)[None, None, :, None]
    weight = jnp.where(cells == offset, 1.0 - fraction, 0.0) + jnp.where(
        cells == offset - 1, fraction, 0.0
    )
    return jnp.pad(weight, ((0, 0), (0, 0), (0, 0), (0, WIDE - SEG)))


def per_device(
    spectral_in, leg_synthesis, leg_analysis, slot_pair, departure_cells, departure_frac
):
    bands, lons = lax.axis_size("band"), lax.axis_size("lon")
    band, lon = lax.axis_index("band"), lax.axis_index("lon")
    slot = (band * lons + lon).astype(jnp.int32).reshape(1)
    outgoing = pl.pallas_call(
        synthesis_kernel,
        out_shape=jax.ShapeDtypeStruct((SLOTS, 256), F32),
        in_specs=[SMEM, SMEM, VMEM, VMEM],
        out_specs=VMEM,
        scratch_shapes=legendre_scratch(),
        compiler_params=PARAMS,
        name="legendre_synthesis",
    )(slot, slot_pair, spectral_in, leg_synthesis)
    arrived = lax.all_to_all(
        outgoing.reshape(SLOTS, 1, 256), ("band", "lon"), split_axis=0, concat_axis=0, tiled=True
    ).reshape(SLOTS, 256)
    choice = slot_choice(slot_pair)
    weights = advection_weights(departure_cells, departure_frac, band, lon, bands)
    (synth_h, synth_l), (anal_h, anal_l), twiddle = fine_tables()
    returning = pl.pallas_call(
        grid_kernel,
        out_shape=jax.ShapeDtypeStruct((SLOTS, 256), F32),
        in_specs=[VMEM] * 8,
        out_specs=VMEM,
        scratch_shapes=[
            pltpu.VMEM((640, 256), F32),
            pltpu.VMEM((320, 2 * WIDE), F32),
            pltpu.VMEM((320, 2 * WIDE), F32),
            pltpu.VMEM((160, 1024), F32),
        ],
        compiler_params=PARAMS,
        name="grid_step",
    )(arrived, choice, weights, synth_h, synth_l, anal_h, anal_l, twiddle)
    returned = lax.all_to_all(
        returning.reshape(SLOTS, 1, 256), ("band", "lon"), split_axis=0, concat_axis=0, tiled=True
    ).reshape(SLOTS, 256)
    return pl.pallas_call(
        analysis_kernel,
        out_shape=jax.ShapeDtypeStruct((1, 32, ROWS), F32),
        in_specs=[SMEM, SMEM, VMEM, VMEM],
        out_specs=VMEM,
        scratch_shapes=legendre_scratch(),
        compiler_params=PARAMS,
        name="legendre_analysis",
    )(slot, slot_pair, returned, leg_analysis)


def solution(mesh):
    return jax.shard_map(
        per_device,
        mesh=mesh,
        in_specs=(
            P(("band", "lon"), None, None),
            P(("band", "lon"), None, None),
            P(("band", "lon"), None, None),
            P(),
            P("band", None),
            P("band", None),
        ),
        out_specs=P(("band", "lon"), None, None),
        check_vma=False,
    )
```

```python
import math

import jax
import jax.numpy as jnp
import ml_dtypes
import numpy as np
from jax import lax
from jax.experimental import pallas as pl
from jax.experimental.pallas import tpu as pltpu
from jax.sharding import PartitionSpec as P

WAVES = 640
PAIRS = 320
ROWS = 641
HALF = 640
NLON = 2560
SLOTS = 512
RADIX = 8
FINE = 80
SEG = 320
WIDE = 384
HALF_ROWS = 5
REACH = 4
BF = jnp.bfloat16
F32 = jnp.float32


def halves(table):
    high = table.astype(np.float32).astype(ml_dtypes.bfloat16)
    low = (table - high.astype(np.float64)).astype(np.float32).astype(ml_dtypes.bfloat16)
    return high, low


def fine_tables():
    place = np.arange(WIDE)
    place = np.where(place < SEG, place, place - WIDE)
    phase = (np.arange(FINE)[:, None] * place[None, :]) % SEG
    cos, sin = np.cos(2 * math.pi * phase / SEG), np.sin(2 * math.pi * phase / SEG)
    synth = np.zeros((256, 2 * WIDE))
    synth[0:FINE, :WIDE] = 2 * cos
    synth[0:FINE, WIDE:] = 2 * sin
    synth[128 : 128 + FINE, :WIDE] = -2 * sin
    synth[128 : 128 + FINE, WIDE:] = 2 * cos
    anal = np.zeros((2 * WIDE, 256))
    anal[:WIDE, 0:FINE] = cos.T / NLON
    anal[WIDE:, 0:FINE] = sin.T / NLON
    anal[:WIDE, 128 : 128 + FINE] = -sin.T / NLON
    anal[WIDE:, 128 : 128 + FINE] = cos.T / NLON
    turn = 2 * math.pi * ((np.arange(RADIX)[:, None] * place[None, :]) % NLON) / NLON
    twiddle = np.concatenate([np.cos(turn), np.sin(turn)], axis=0).astype(np.float32)
    return halves(synth), halves(anal), twiddle


def split(value):
    high = value.astype(BF)
    return high, (value - high.astype(F32)).astype(BF)


def dot3(left, right_high, right_low):
    high, low = split(left)
    rows = left.shape[0]
    both = jnp.dot(
        jnp.concatenate([high, low], axis=0), right_high, preferred_element_type=F32
    )
    return both[:rows] + both[rows:] + jnp.dot(high, right_low, preferred_element_type=F32)


def wave_rows(pair):
    row = lax.broadcasted_iota(jnp.int32, (1, ROWS), 1)
    cut = WAVES - pair
    upper = row < cut
    odd = jnp.where(upper, row, row - cut) & 1
    return upper, odd


def synthesis_kernel(slot_ref, pairs_ref, spec_ref, table_ref, out_ref, turned, south):
    pair = pairs_ref[slot_ref[0]]
    upper, odd = wave_rows(pair)
    live = pair < PAIRS
    groups = []
    for parity in range(2):
        for half in range(2):
            for wave in range(2):
                mask = jnp.logical_and(upper if wave == 0 else jnp.logical_not(upper), odd == parity)
                mask = jnp.logical_and(mask, live)
                for part in range(2):
                    first = part * 16 + half * 8
                    groups.append(jnp.where(mask, spec_ref[0, first : first + 8, :], 0.0))
    table_high, table_low = split(table_ref[0])
    product = dot3(jnp.concatenate(groups, axis=0), table_high, table_low)
    even, odd_sum = product[:64], product[64:]
    turned[...] = jnp.concatenate([even + odd_sum, even - odd_sum], axis=0).T
    lane = lax.broadcasted_iota(jnp.int32, (128, 128), 1)
    left = lane < 64
    pick = [turned[pl.ds(u, 128, stride=5), :] for u in range(5)]
    rolled = [pltpu.roll(q, 64, 1) for q in pick]
    out_ref[pl.ds(0, 128, stride=4), :] = jnp.where(left, pick[0], rolled[1])
    out_ref[pl.ds(1, 128, stride=4), :] = pick[2]
    out_ref[pl.ds(2, 128, stride=4), :] = jnp.where(left, pick[3], rolled[4])
    out_ref[pl.ds(3, 128, stride=4), :] = pltpu.roll(pick[2], 96, 1)
    south[pl.ds(0, 128, stride=4), :] = jnp.where(left, rolled[0], pick[1])
    south[pl.ds(1, 128, stride=4), :] = rolled[2]
    south[pl.ds(2, 128, stride=4), :] = jnp.where(left, rolled[3], pick[4])
    south[pl.ds(3, 128, stride=4), :] = pltpu.roll(pick[2], 32, 1)
    for block in range(32):
        at = (63 - block) * 16
        out_ref[at : at + 16, :] = south[block * 16 : block * 16 + 16, :]


def grid_kernel(
    in_ref, choice_ref, weight_ref, synth_h, synth_l, anal_h, anal_l, twiddle_ref, out_ref,
    coeff, spread, fields, back
):
    columns = jnp.concatenate(
        [in_ref[pl.ds(0, SLOTS, stride=2), :].T, in_ref[pl.ds(1, SLOTS, stride=2), :].T[:32]], axis=0
    )
    high, low = split(columns)
    picked = jnp.dot(
        jnp.concatenate([high, low], axis=0), choice_ref[...], preferred_element_type=F32
    )
    lane = lax.broadcasted_iota(jnp.int32, (8, 128), 1)
    first_wave = lane < FINE // 2
    mean_scale = jnp.where(lane == 0, 0.5, 1.0)
    for level in range(2):
        for i in range(HALF_ROWS):
            for r in range(RADIX):
                for part in range(2):
                    base = level * 160 + i * 32 + part * 8
                    value = jnp.where(
                        first_wave,
                        picked[base : base + 8, r * 128 : r * 128 + 128],
                        picked[base + 16 : base + 24, r * 128 : r * 128 + 128],
                    )
                    if r == 0:
                        value = value * mean_scale
                    at = level * 320 + i * 64 + r * 8
                    coeff[at : at + 8, part * 128 : part * 128 + 128] = value
    both = coeff[...].astype(BF)
    wide = jnp.dot(both, synth_h[...], preferred_element_type=F32)
    spread[...] = (
        wide[:320] + wide[320:] + jnp.dot(both[:320], synth_l[...], preferred_element_type=F32)
    )
    root = math.sqrt(0.5)
    for i in range(HALF_ROWS):
        real, imag = [], []
        for r in range(RADIX):
            at = i * 64 + r * 8
            zr, zi = spread[at : at + 8, :WIDE], spread[at : at + 8, WIDE:]
            if r == 0:
                real.append(zr)
                imag.append(None)
                continue
            tr, ti = twiddle_ref[r : r + 1, :], twiddle_ref[RADIX + r : RADIX + r + 1, :]
            real.append(tr * zr - ti * zi)
            imag.append(None if r == 4 else tr * zi + ti * zr)
        plus, minus = real[0] + real[4], real[0] - real[4]
        p, n = real[2] + real[6], imag[2] - imag[6]
        evens = [plus + p, minus - n, plus - p, minus + n]
        a, b = real[1] + real[7], real[3] + real[5]
        c, d = imag[1] - imag[7], imag[3] - imag[5]
        odds = [a + b, root * ((a - b) - (c + d)), d - c, -root * ((a - b) + (c + d))]
        moved = []
        for k in range(RADIX):
            value = evens[k] + odds[k] if k < 4 else evens[k - 4] - odds[k - 4]
            total = weight_ref[i, k, 0:1, :] * value
            for offset in range(1, REACH + 1):
                total = total + weight_ref[i, k, offset : offset + 1, :] * pltpu.roll(
                    value, offset, 1
                )
            moved.append(total)
        s = [moved[k] + moved[k + 4] for k in range(4)]
        d = [moved[k] - moved[k + 4] for k in range(4)]
        s02, s13 = s[0] + s[2], s[1] + s[3]
        dd, ds = root * (d[1] - d[3]), root * (d[1] + d[3])
        waves = [
            (s02 + s13, None),
            (d[0] + dd, -d[2] - ds),
            (s[0] - s[2], s[3] - s[1]),
            (d[0] - dd, d[2] - ds),
            (s02 - s13, None),
        ]
        for r in range(RADIX):
            vr, vi = waves[r] if r < 5 else waves[8 - r]
            if r > 4:
                vi = -vi
            at = i * 64 + r * 8
            if r == 0:
                fields[at : at + 8, :WIDE] = vr
                fields[at : at + 8, WIDE:] = jnp.zeros_like(vr)
                continue
            tr, ti = twiddle_ref[r : r + 1, :], twiddle_ref[RADIX + r : RADIX + r + 1, :]
            if vi is None:
                fields[at : at + 8, :WIDE] = tr * vr
                fields[at : at + 8, WIDE:] = -ti * vr
            else:
                fields[at : at + 8, :WIDE] = tr * vr + ti * vi
                fields[at : at + 8, WIDE:] = tr * vi - ti * vr
    result = dot3(fields[...], anal_h[...], anal_l[...])
    for i in range(HALF_ROWS):
        for r in range(RADIX):
            for part in range(2):
                at = i * 64 + r * 8
                value = result[at : at + 8, part * 128 : part * 128 + 128]
                base = i * 32 + part * 8
                back[base : base + 8, r * 128 : r * 128 + 128] = jnp.where(first_wave, value, 0.0)
                back[base + 16 : base + 24, r * 128 : r * 128 + 128] = jnp.where(
                    first_wave, 0.0, value
                )
    high, low = split(back[...])
    across = (((1,), (1,)), ((), ()))
    choice = choice_ref[...]
    message = lax.dot_general(
        choice, high, across, preferred_element_type=F32
    ) + lax.dot_general(choice, low, across, preferred_element_type=F32)
    out_ref[pl.ds(0, SLOTS, stride=2), :] = message[:, 0:128]
    out_ref[pl.ds(1, SLOTS, stride=2), 0:32] = message[:, 128:160]


def analysis_kernel(slot_ref, pairs_ref, in_ref, table_ref, out_ref, turned, south):
    for block in range(32):
        at = (63 - block) * 16
        south[block * 16 : block * 16 + 16, :] = in_ref[at : at + 16, :]
    lane = lax.broadcasted_iota(jnp.int32, (128, 128), 1)
    left = lane < 64
    north_a, north_b = ([in_ref[pl.ds(2 * f + c, 128, stride=4), :] for f in range(2)] for c in range(2))
    south_a, south_b = ([south[pl.ds(2 * f + c, 128, stride=4), :] for f in range(2)] for c in range(2))
    for f in range(2):
        turned[pl.ds(3 * f, 128, stride=5), :] = jnp.where(
            left, north_a[f], pltpu.roll(south_a[f], 64, 1)
        )
        turned[pl.ds(3 * f + 1, 128, stride=5), :] = jnp.where(
            left, pltpu.roll(north_a[f], 64, 1), south_a[f]
        )
    turned[pl.ds(2, 128, stride=5), :] = jnp.where(
        left,
        jnp.where(lane < 32, north_b[0], pltpu.roll(north_b[1], 32, 1)),
        jnp.where(lane < 96, pltpu.roll(south_b[0], 64, 1), pltpu.roll(south_b[1], 96, 1)),
    )
    straight = turned[...].T
    north, south_rows = straight[:64], straight[64:]
    table_high, table_low = split(table_ref[0])
    product = dot3(
        jnp.concatenate([north + south_rows, north - south_rows], axis=0), table_high, table_low
    )
    pair = pairs_ref[slot_ref[0]]
    upper, odd = wave_rows(pair)
    live = pair < PAIRS
    even = odd == 0
    for half in range(2):
        for part in range(2):
            rows = [
                [
                    product[
                        parity * 64 + half * 32 + wave * 16 + part * 8 :
                        parity * 64 + half * 32 + wave * 16 + part * 8 + 8
                    ]
                    for parity in range(2)
                ]
                for wave in range(2)
            ]
            value = jnp.where(
                upper,
                jnp.where(even, rows[0][0], rows[0][1]),
                jnp.where(even, rows[1][0], rows[1][1]),
            )
            first = part * 16 + half * 8
            out_ref[0, first : first + 8, :] = jnp.where(live, value, 0.0)


SMEM = pl.BlockSpec(memory_space=pltpu.SMEM)
VMEM = pl.BlockSpec(memory_space=pltpu.VMEM)
PARAMS = pltpu.CompilerParams(vmem_limit_bytes=40 * 1024 * 1024)


def legendre_scratch():
    return [pltpu.VMEM((HALF, 128), F32), pltpu.VMEM((512, 128), F32)]


def slot_choice(slot_pair):
    block = jnp.arange(RADIX * 128, dtype=jnp.int32)
    fine, rest = block % 128, block // 128
    wave = fine * RADIX + rest
    pair = jnp.where(wave < PAIRS, wave, WAVES - 1 - wave)
    pair = jnp.where(fine < FINE, pair, -1)
    return (slot_pair[:, None] == pair[None, :]).astype(BF)


def advection_weights(cells, fraction, band, lon, bands):
    position = jnp.arange(HALF_ROWS, dtype=jnp.int32)
    position = jnp.where(lon % 2 == 0, position, (position + 1) % HALF_ROWS)
    row = (HALF_ROWS * lon + position) // 2
    row = jnp.where(band < bands // 2, row, cells.shape[0] - 1 - row)
    cells = jnp.take(cells, row, axis=0).reshape(HALF_ROWS, RADIX, 1, SEG)
    fraction = jnp.take(fraction, row, axis=0).reshape(HALF_ROWS, RADIX, 1, SEG)
    offset = jnp.arange(REACH + 1, dtype=jnp.int32)[None, None, :, None]
    weight = jnp.where(cells == offset, 1.0 - fraction, 0.0) + jnp.where(
        cells == offset - 1, fraction, 0.0
    )
    return jnp.pad(weight, ((0, 0), (0, 0), (0, 0), (0, WIDE - SEG)))


def per_device(
    spectral_in, leg_synthesis, leg_analysis, slot_pair, departure_cells, departure_frac
):
    bands, lons = lax.axis_size("band"), lax.axis_size("lon")
    band, lon = lax.axis_index("band"), lax.axis_index("lon")
    slot = (band * lons + lon).astype(jnp.int32).reshape(1)
    outgoing = pl.pallas_call(
        synthesis_kernel,
        out_shape=jax.ShapeDtypeStruct((2 * SLOTS, 128), F32),
        in_specs=[SMEM, SMEM, VMEM, VMEM],
        out_specs=VMEM,
        scratch_shapes=legendre_scratch(),
        compiler_params=PARAMS,
        name="legendre_synthesis",
    )(slot, slot_pair, spectral_in, leg_synthesis)
    arrived = lax.all_to_all(
        outgoing.reshape(SLOTS, 2, 128), ("band", "lon"), split_axis=0, concat_axis=0, tiled=True
    ).reshape(2 * SLOTS, 128)
    choice = slot_choice(slot_pair)
    weights = advection_weights(departure_cells, departure_frac, band, lon, bands)
    (synth_h, synth_l), (anal_h, anal_l), twiddle = fine_tables()
    returning = pl.pallas_call(
        grid_kernel,
        out_shape=jax.ShapeDtypeStruct((2 * SLOTS, 128), F32),
        in_specs=[VMEM] * 8,
        out_specs=VMEM,
        scratch_shapes=[
            pltpu.VMEM((640, 256), F32),
            pltpu.VMEM((320, 2 * WIDE), F32),
            pltpu.VMEM((320, 2 * WIDE), F32),
            pltpu.VMEM((160, 1024), F32),
        ],
        compiler_params=PARAMS,
        name="grid_step",
    )(arrived, choice, weights, synth_h, synth_l, anal_h, anal_l, twiddle)
    returned = lax.all_to_all(
        returning.reshape(SLOTS, 2, 128), ("band", "lon"), split_axis=0, concat_axis=0, tiled=True
    ).reshape(2 * SLOTS, 128)
    return pl.pallas_call(
        analysis_kernel,
        out_shape=jax.ShapeDtypeStruct((1, 32, ROWS), F32),
        in_specs=[SMEM, SMEM, VMEM, VMEM],
        out_specs=VMEM,
        scratch_shapes=legendre_scratch(),
        compiler_params=PARAMS,
        name="legendre_analysis",
    )(slot, slot_pair, returned, leg_analysis)


def solution(mesh):
    return jax.shard_map(
        per_device,
        mesh=mesh,
        in_specs=(
            P(("band", "lon"), None, None),
            P(("band", "lon"), None, None),
            P(("band", "lon"), None, None),
            P(),
            P("band", None),
            P("band", None),
        ),
        out_specs=P(("band", "lon"), None, None),
        check_vma=False,
    )
```

```python
import math

import jax
import jax.numpy as jnp
import ml_dtypes
import numpy as np
from jax import lax
from jax.experimental import pallas as pl
from jax.experimental.pallas import tpu as pltpu
from jax.sharding import PartitionSpec as P

WAVES = 640
PAIRS = 320
ROWS = 641
HALF = 640
NLON = 2560
SLOTS = 512
RADIX = 10
FINE = 64
SEG = 256
HALF_ROWS = 5
REACH = 4
BF = jnp.bfloat16
F32 = jnp.float32


def halves(table):
    high = table.astype(np.float32).astype(ml_dtypes.bfloat16)
    low = (table - high.astype(np.float64)).astype(np.float32).astype(ml_dtypes.bfloat16)
    return high, low


def fine_tables():
    place = np.arange(SEG)
    phase = 2 * math.pi * ((np.arange(FINE)[:, None] * place[None, :]) % SEG) / SEG
    cos, sin = np.cos(phase), np.sin(phase)
    synth = np.block([[2 * cos, 2 * sin], [-2 * sin, 2 * cos]])
    high, low = halves(synth)
    anal_high, anal_low = halves(synth.T / (2 * NLON))
    turn = 2 * math.pi * ((np.arange(RADIX)[:, None] * place[None, :]) % NLON) / NLON
    twiddle = np.concatenate([np.cos(turn), np.sin(turn)], axis=0).astype(np.float32)
    return (
        np.concatenate([high, high, low], axis=0),
        np.concatenate([anal_high, anal_low], axis=1),
        twiddle,
    )


def split(value):
    high = value.astype(BF)
    return high, (value - high.astype(F32)).astype(BF)


def dot3(left, right_high, right_low):
    high, low = split(left)
    rows = left.shape[0]
    both = jnp.dot(
        jnp.concatenate([high, low], axis=0), right_high, preferred_element_type=F32
    )
    return both[:rows] + both[rows:] + jnp.dot(high, right_low, preferred_element_type=F32)


def wave_rows(pair):
    row = lax.broadcasted_iota(jnp.int32, (1, ROWS), 1)
    cut = WAVES - pair
    upper = row < cut
    odd = jnp.where(upper, row, row - cut) & 1
    return upper, odd


def own_pair(pairs_ref):
    slot = lax.axis_index("band") * lax.axis_size("lon") + lax.axis_index("lon")
    shape = pairs_ref.shape
    index = lax.broadcasted_iota(jnp.int32, shape, 0) * shape[1] + lax.broadcasted_iota(
        jnp.int32, shape, 1
    )
    mine = jnp.where(index == slot, pairs_ref[...], 0)
    return jnp.sum(jnp.sum(mine, axis=1, keepdims=True), axis=0, keepdims=True)


def synthesis_kernel(pairs_ref, spec_ref, table_ref, out_ref, turned, south):
    pair = own_pair(pairs_ref)
    upper, odd = wave_rows(pair)
    live = pair < PAIRS
    groups = []
    for parity in range(2):
        for half in range(2):
            for wave in range(2):
                mask = jnp.logical_and(upper if wave == 0 else jnp.logical_not(upper), odd == parity)
                mask = jnp.logical_and(mask, live)
                for part in range(2):
                    first = part * 16 + half * 8
                    groups.append(jnp.where(mask, spec_ref[0, first : first + 8, :], 0.0))
    table_high, table_low = split(table_ref[0])
    product = dot3(jnp.concatenate(groups, axis=0), table_high, table_low)
    even, odd_sum = product[:64], product[64:]
    turned[...] = jnp.concatenate([even + odd_sum, even - odd_sum], axis=0).T
    lane = lax.broadcasted_iota(jnp.int32, (128, 128), 1)
    left = lane < 64
    pick = [turned[pl.ds(u, 128, stride=5), :] for u in range(5)]
    rolled = [pltpu.roll(q, 64, 1) for q in pick]
    out_ref[pl.ds(0, 128, stride=4), :] = jnp.where(left, pick[0], rolled[1])
    out_ref[pl.ds(1, 128, stride=4), :] = pick[2]
    out_ref[pl.ds(2, 128, stride=4), :] = jnp.where(left, pick[3], rolled[4])
    out_ref[pl.ds(3, 128, stride=4), :] = pltpu.roll(pick[2], 96, 1)
    south[pl.ds(0, 128, stride=4), :] = jnp.where(left, rolled[0], pick[1])
    south[pl.ds(1, 128, stride=4), :] = rolled[2]
    south[pl.ds(2, 128, stride=4), :] = jnp.where(left, rolled[3], pick[4])
    south[pl.ds(3, 128, stride=4), :] = pltpu.roll(pick[2], 32, 1)
    for block in range(32):
        at = (63 - block) * 16
        out_ref[at : at + 16, :] = south[block * 16 : block * 16 + 16, :]


def circle(degrees):
    return math.cos(math.radians(degrees)), math.sin(math.radians(degrees))


COS36, SIN36 = circle(36)
COS72, SIN72 = circle(72)


def to_segments(real, imag):
    p1, p2 = real[2] + real[8], real[4] + real[6]
    n1, n2 = imag[2] - imag[8], imag[4] - imag[6]
    a1, b1 = real[0] + COS72 * p1 - COS36 * p2, SIN72 * n1 + SIN36 * n2
    a2, b2 = real[0] - COS36 * p1 + COS72 * p2, SIN36 * n1 - SIN72 * n2
    evens = [real[0] + p1 + p2, a1 - b1, a2 - b2, a2 + b2, a1 + b1]
    q1, q3 = real[1] + real[9], real[3] + real[7]
    h1, h3 = imag[1] - imag[9], imag[3] - imag[7]
    a1, b1 = COS36 * q1 - COS72 * q3 - real[5], SIN36 * h1 + SIN72 * h3
    a2, b2 = real[5] + COS72 * q1 - COS36 * q3, SIN72 * h1 - SIN36 * h3
    odds = [real[5] + q1 + q3, a1 - b1, a2 - b2, -a2 - b2, -a1 - b1]
    return [e + o for e, o in zip(evens, odds)] + [e - o for e, o in zip(evens, odds)]


def from_segments(parts):
    s = [parts[k] + parts[k + 5] for k in range(5)]
    d = [parts[k] - parts[k + 5] for k in range(5)]
    p1, p2, n1, n2 = s[1] + s[4], s[2] + s[3], s[1] - s[4], s[2] - s[3]
    q1, q2, h1, h2 = d[1] - d[4], d[2] - d[3], d[1] + d[4], d[2] + d[3]
    return [
        (s[0] + p1 + p2, None),
        (d[0] + COS36 * q1 + COS72 * q2, -SIN36 * h1 - SIN72 * h2),
        (s[0] + COS72 * p1 - COS36 * p2, -SIN72 * n1 - SIN36 * n2),
        (d[0] - COS72 * q1 - COS36 * q2, SIN36 * h2 - SIN72 * h1),
        (s[0] - COS36 * p1 + COS72 * p2, SIN72 * n2 - SIN36 * n1),
        (d[0] - q1 + q2, None),
    ]


def grid_kernel(
    in_ref, choice_ref, weight_ref, synth_ref, anal_ref, twiddle_ref, out_ref,
    coeff, spread, fields, back
):
    columns = jnp.concatenate(
        [in_ref[pl.ds(0, SLOTS, stride=2), :].T, in_ref[pl.ds(1, SLOTS, stride=2), :].T[:32]], axis=0
    )
    choice = choice_ref[...]
    picked = jnp.dot(
        jnp.concatenate(split(columns), axis=0), choice, preferred_element_type=F32
    )
    lane = lax.broadcasted_iota(jnp.int32, (8, 128), 1)
    left = lane < FINE
    first_wave = (lane & (FINE - 1)) < FINE // 2
    mean_scale = jnp.where((lane & (FINE - 1)) == 0, 0.5, 1.0)
    for level in range(2):
        for i in range(HALF_ROWS):
            for q in range(RADIX // 2):
                base, cols = level * 160 + i * 32, slice(q * 128, q * 128 + 128)
                real = jnp.where(
                    first_wave, picked[base : base + 8, cols], picked[base + 16 : base + 24, cols]
                )
                imag = jnp.where(
                    first_wave, picked[base + 8 : base + 16, cols], picked[base + 24 : base + 32, cols]
                )
                even = jnp.where(left, real, pltpu.roll(imag, 64, 1))
                odd = jnp.where(left, pltpu.roll(real, 64, 1), imag)
                if q == 0:
                    even = even * mean_scale
                at = i * 80 + q * 16
                coeff[at : at + 8, level * 128 : level * 128 + 128] = even
                coeff[at + 8 : at + 16, level * 128 : level * 128 + 128] = odd
    both = coeff[...].astype(BF)
    spread[...] = jnp.dot(
        jnp.concatenate([both, both[:, :128]], axis=1), synth_ref[...], preferred_element_type=F32
    )
    for i in range(HALF_ROWS):
        real, imag = [], []
        for r in range(RADIX):
            at = i * 80 + r * 8
            zr, zi = spread[at : at + 8, :SEG], spread[at : at + 8, SEG:]
            if r == 0:
                real.append(zr)
                imag.append(None)
                continue
            tr, ti = twiddle_ref[r : r + 1, :], twiddle_ref[RADIX + r : RADIX + r + 1, :]
            real.append(tr * zr - ti * zi)
            imag.append(None if r == 5 else tr * zi + ti * zr)
        value = jnp.concatenate(to_segments(real, imag), axis=1)
        moved = weight_ref[i, 0:1, :] * value
        for offset in range(1, REACH + 1):
            moved = moved + weight_ref[i, offset : offset + 1, :] * pltpu.roll(value, offset, 1)
        waves = from_segments([moved[:, k * SEG : k * SEG + SEG] for k in range(RADIX)])
        for r in range(RADIX):
            vr, vi = waves[r] if r < 6 else waves[RADIX - r]
            if r > 5:
                vi = -vi
            at = i * 80 + r * 8
            if r == 0:
                fields[at : at + 8, :SEG] = vr
                fields[at : at + 8, SEG:] = jnp.zeros_like(vr)
                continue
            tr, ti = twiddle_ref[r : r + 1, :], twiddle_ref[RADIX + r : RADIX + r + 1, :]
            if vi is None:
                fields[at : at + 8, :SEG] = tr * vr
                fields[at : at + 8, SEG:] = -ti * vr
            else:
                fields[at : at + 8, :SEG] = tr * vr + ti * vi
                fields[at : at + 8, SEG:] = tr * vi - ti * vr
    wide = jnp.dot(
        jnp.concatenate(split(fields[...]), axis=0), anal_ref[...], preferred_element_type=F32
    )
    result = wide[:400, :128] + wide[:400, 128:] + wide[400:, :128]
    for i in range(HALF_ROWS):
        for q in range(RADIX // 2):
            at, cols = i * 80 + q * 16, slice(q * 128, q * 128 + 128)
            even, odd = result[at : at + 8], result[at + 8 : at + 16]
            real = jnp.where(left, even, pltpu.roll(odd, 64, 1))
            imag = jnp.where(left, pltpu.roll(even, 64, 1), odd)
            base = i * 32
            back[base : base + 8, cols] = jnp.where(first_wave, real, 0.0)
            back[base + 8 : base + 16, cols] = jnp.where(first_wave, imag, 0.0)
            back[base + 16 : base + 24, cols] = jnp.where(first_wave, 0.0, real)
            back[base + 24 : base + 32, cols] = jnp.where(first_wave, 0.0, imag)
    sent = lax.dot_general(
        jnp.concatenate(split(back[...]), axis=0), choice, (((1,), (1,)), ((), ())),
        preferred_element_type=F32,
    )
    sent = sent[:160] + sent[160:]
    out_ref[pl.ds(0, SLOTS, stride=2), :] = sent[:128].T
    out_ref[pl.ds(1, SLOTS, stride=2), 0:32] = sent[128:].T


def analysis_kernel(pairs_ref, in_ref, table_ref, out_ref, turned, south):
    for block in range(32):
        at = (63 - block) * 16
        south[block * 16 : block * 16 + 16, :] = in_ref[at : at + 16, :]
    lane = lax.broadcasted_iota(jnp.int32, (128, 128), 1)
    left = lane < 64
    north_a, north_b = ([in_ref[pl.ds(2 * f + c, 128, stride=4), :] for f in range(2)] for c in range(2))
    south_a, south_b = ([south[pl.ds(2 * f + c, 128, stride=4), :] for f in range(2)] for c in range(2))
    for f in range(2):
        turned[pl.ds(3 * f, 128, stride=5), :] = jnp.where(
            left, north_a[f], pltpu.roll(south_a[f], 64, 1)
        )
        turned[pl.ds(3 * f + 1, 128, stride=5), :] = jnp.where(
            left, pltpu.roll(north_a[f], 64, 1), south_a[f]
        )
    turned[pl.ds(2, 128, stride=5), :] = jnp.where(
        left,
        jnp.where(lane < 32, north_b[0], pltpu.roll(north_b[1], 32, 1)),
        jnp.where(lane < 96, pltpu.roll(south_b[0], 64, 1), pltpu.roll(south_b[1], 96, 1)),
    )
    straight = turned[...].T
    north, south_rows = straight[:64], straight[64:]
    table_high, table_low = split(table_ref[0])
    product = dot3(
        jnp.concatenate([north + south_rows, north - south_rows], axis=0), table_high, table_low
    )
    pair = own_pair(pairs_ref)
    upper, odd = wave_rows(pair)
    live = pair < PAIRS
    even = odd == 0
    for half in range(2):
        for part in range(2):
            rows = [
                [
                    product[
                        parity * 64 + half * 32 + wave * 16 + part * 8 :
                        parity * 64 + half * 32 + wave * 16 + part * 8 + 8
                    ]
                    for parity in range(2)
                ]
                for wave in range(2)
            ]
            value = jnp.where(
                upper,
                jnp.where(even, rows[0][0], rows[0][1]),
                jnp.where(even, rows[1][0], rows[1][1]),
            )
            first = part * 16 + half * 8
            out_ref[0, first : first + 8, :] = jnp.where(live, value, 0.0)


VMEM = pl.BlockSpec(memory_space=pltpu.VMEM)
PARAMS = pltpu.CompilerParams(vmem_limit_bytes=40 * 1024 * 1024)


def slot_choice(slot_pair):
    column = jnp.arange(RADIX * FINE, dtype=jnp.int32)
    wave = (column % FINE) * RADIX + column // FINE
    pair = jnp.where(wave < PAIRS, wave, WAVES - 1 - wave)
    return (slot_pair[:, None] == pair[None, :]).astype(BF)


def advection_weights(cells, fraction, band, lon, bands):
    position = jnp.arange(HALF_ROWS, dtype=jnp.int32)
    position = jnp.where(lon % 2 == 0, position, (position + 1) % HALF_ROWS)
    row = (HALF_ROWS * lon + position) // 2
    row = jnp.where(band < bands // 2, row, cells.shape[0] - 1 - row)
    cells = jnp.take(cells, row, axis=0)[:, None, :]
    fraction = jnp.take(fraction, row, axis=0)[:, None, :]
    offset = jnp.arange(REACH + 1, dtype=jnp.int32)[None, :, None]
    return jnp.where(cells == offset, 1.0 - fraction, 0.0) + jnp.where(
        cells == offset - 1, fraction, 0.0
    )


def legendre_synthesis(slot_pair, spectral_in, leg_synthesis):
    return pl.pallas_call(
        synthesis_kernel,
        out_shape=jax.ShapeDtypeStruct((2 * SLOTS, 128), F32),
        in_specs=[VMEM] * 3,
        out_specs=VMEM,
        scratch_shapes=[
            pltpu.VMEM((HALF, 128), F32),
            pltpu.VMEM((SLOTS, 128), F32),
        ],
        compiler_params=PARAMS,
        name="legendre_synthesis",
    )(slot_pair.reshape(-1, 128), spectral_in, leg_synthesis)


def grid_step(arrived, choice, weights):
    return pl.pallas_call(
        grid_kernel,
        out_shape=jax.ShapeDtypeStruct((2 * SLOTS, 128), F32),
        in_specs=[VMEM] * 6,
        out_specs=VMEM,
        scratch_shapes=[
            pltpu.VMEM((400, 256), F32),
            pltpu.VMEM((400, 2 * SEG), F32),
            pltpu.VMEM((400, 2 * SEG), F32),
            pltpu.VMEM((160, WAVES), F32),
        ],
        compiler_params=PARAMS,
        name="grid_step",
    )(arrived, choice, weights, *fine_tables())


def legendre_analysis(slot_pair, returned, leg_analysis):
    return pl.pallas_call(
        analysis_kernel,
        out_shape=jax.ShapeDtypeStruct((1, 32, ROWS), F32),
        in_specs=[VMEM] * 3,
        out_specs=VMEM,
        scratch_shapes=[pltpu.VMEM((HALF, 128), F32), pltpu.VMEM((SLOTS, 128), F32)],
        compiler_params=PARAMS,
        name="legendre_analysis",
    )(slot_pair.reshape(-1, 128), returned, leg_analysis)


def exchange(messages):
    return lax.all_to_all(
        messages.reshape(SLOTS, 2, 128), ("band", "lon"), split_axis=0, concat_axis=0, tiled=True
    ).reshape(2 * SLOTS, 128)


def per_device(
    spectral_in, leg_synthesis, leg_analysis, slot_pair, departure_cells, departure_frac
):
    arrived = exchange(legendre_synthesis(slot_pair, spectral_in, leg_synthesis))
    choice = slot_choice(slot_pair)
    weights = advection_weights(
        departure_cells, departure_frac, lax.axis_index("band"), lax.axis_index("lon"),
        lax.axis_size("band"),
    )
    returned = exchange(grid_step(arrived, choice, weights))
    return legendre_analysis(slot_pair, returned, leg_analysis)


def solution(mesh):
    return jax.shard_map(
        per_device,
        mesh=mesh,
        in_specs=(
            P(("band", "lon"), None, None),
            P(("band", "lon"), None, None),
            P(("band", "lon"), None, None),
            P(),
            P("band", None),
            P("band", None),
        ),
        out_specs=P(("band", "lon"), None, None),
        check_vma=False,
    )
```

```python
import math

import jax
import jax.numpy as jnp
import ml_dtypes
import numpy as np
from jax import lax
from jax.experimental import pallas as pl
from jax.experimental.pallas import tpu as pltpu
from jax.sharding import PartitionSpec as P

WAVES = 640
PAIRS = 320
ROWS = 641
HALF = 640
NLON = 2560
SLOTS = 512
RADIX = 10
FINE = 64
SEG = 256
HALF_ROWS = 5
REACH = 4
BF = jnp.bfloat16
F32 = jnp.float32


def halves(table):
    high = table.astype(np.float32).astype(ml_dtypes.bfloat16)
    low = (table - high.astype(np.float64)).astype(np.float32).astype(ml_dtypes.bfloat16)
    return high, low


def fine_tables():
    place = np.arange(SEG)
    phase = 2 * math.pi * ((np.arange(FINE)[:, None] * place[None, :]) % SEG) / SEG
    cos, sin = np.cos(phase), np.sin(phase)
    synth = np.block([[2 * cos, 2 * sin], [-2 * sin, 2 * cos]])
    high, low = halves(synth)
    anal_high, anal_low = halves(synth.T / (2 * NLON))
    turn = 2 * math.pi * ((np.arange(RADIX)[:, None] * place[None, :]) % NLON) / NLON
    twiddle = np.concatenate([np.cos(turn), np.sin(turn)], axis=0).astype(np.float32)
    return (
        np.concatenate([high, high, low], axis=0),
        np.concatenate([anal_high, anal_low], axis=1),
        twiddle,
    )


def split(value):
    high = value.astype(BF)
    return high, (value - high.astype(F32)).astype(BF)


def dot3(left, right_high, right_low):
    high, low = split(left)
    rows = left.shape[0]
    both = jnp.dot(
        jnp.concatenate([high, low], axis=0), right_high, preferred_element_type=F32
    )
    return both[:rows] + both[rows:] + jnp.dot(high, right_low, preferred_element_type=F32)


def wave_rows(pair):
    row = lax.broadcasted_iota(jnp.int32, (1, ROWS), 1)
    cut = WAVES - pair
    upper = row < cut
    odd = jnp.where(upper, row, row - cut) & 1
    return upper, odd


def own_pair(pairs_ref):
    slot = lax.axis_index("band") * lax.axis_size("lon") + lax.axis_index("lon")
    shape = pairs_ref.shape
    index = lax.broadcasted_iota(jnp.int32, shape, 0) * shape[1] + lax.broadcasted_iota(
        jnp.int32, shape, 1
    )
    mine = jnp.where(index == slot, pairs_ref[...], 0)
    return jnp.sum(jnp.sum(mine, axis=1, keepdims=True), axis=0, keepdims=True)


def backwards(value):
    row = lax.broadcasted_iota(jnp.int32, (8, 128), 0)
    parts = [
        jnp.take_along_axis(value[at : at + 8], 7 - row, axis=0, mode="promise_in_bounds")
        for at in range(value.shape[0] - 8, -1, -8)
    ]
    return jnp.concatenate(parts, axis=0)


def synthesis_kernel(pairs_ref, spec_ref, table_ref, out_ref, turned):
    pair = own_pair(pairs_ref)
    upper, odd = wave_rows(pair)
    live = pair < PAIRS
    groups = []
    for parity in range(2):
        for half in range(2):
            for wave in range(2):
                mask = jnp.logical_and(upper if wave == 0 else jnp.logical_not(upper), odd == parity)
                mask = jnp.logical_and(mask, live)
                for part in range(2):
                    first = part * 16 + half * 8
                    groups.append(jnp.where(mask, spec_ref[0, first : first + 8, :], 0.0))
    table_high, table_low = split(table_ref[0])
    product = dot3(jnp.concatenate(groups, axis=0), table_high, table_low)
    even, odd_sum = product[:64], product[64:]
    turned[...] = jnp.concatenate([even + odd_sum, even - odd_sum], axis=0).T
    lane = lax.broadcasted_iota(jnp.int32, (32, 128), 1)
    left = lane < 64
    for g in range(4):
        pick = [turned[pl.ds(5 * g + u, 32, stride=20), :] for u in range(5)]
        rolled = [pltpu.roll(q, 64, 1) for q in pick]
        for f in range(2):
            at = (2 * g + f) * 128
            out_ref[pl.ds(at, 32, stride=2), :] = jnp.where(left, pick[3 * f], rolled[3 * f + 1])
            out_ref[pl.ds(at + 1, 32, stride=2), :] = pltpu.roll(pick[2], 96, 1) if f else pick[2]
            out_ref[pl.ds(at + 64, 32, stride=2), :] = backwards(
                jnp.where(left, rolled[3 * f], pick[3 * f + 1])
            )
            out_ref[pl.ds(at + 65, 32, stride=2), :] = backwards(
                pltpu.roll(pick[2], 32, 1) if f else rolled[2]
            )


def circle(degrees):
    return math.cos(math.radians(degrees)), math.sin(math.radians(degrees))


COS36, SIN36 = circle(36)
COS72, SIN72 = circle(72)


def to_segments(real, imag):
    p1, p2 = real[2] + real[8], real[4] + real[6]
    n1, n2 = imag[2] - imag[8], imag[4] - imag[6]
    a1, b1 = real[0] + COS72 * p1 - COS36 * p2, SIN72 * n1 + SIN36 * n2
    a2, b2 = real[0] - COS36 * p1 + COS72 * p2, SIN36 * n1 - SIN72 * n2
    evens = [real[0] + p1 + p2, a1 - b1, a2 - b2, a2 + b2, a1 + b1]
    q1, q3 = real[1] + real[9], real[3] + real[7]
    h1, h3 = imag[1] - imag[9], imag[3] - imag[7]
    a1, b1 = COS36 * q1 - COS72 * q3 - real[5], SIN36 * h1 + SIN72 * h3
    a2, b2 = real[5] + COS72 * q1 - COS36 * q3, SIN72 * h1 - SIN36 * h3
    odds = [real[5] + q1 + q3, a1 - b1, a2 - b2, -a2 - b2, -a1 - b1]
    return [e + o for e, o in zip(evens, odds)] + [e - o for e, o in zip(evens, odds)]


def from_segments(parts):
    s = [parts[k] + parts[k + 5] for k in range(5)]
    d = [parts[k] - parts[k + 5] for k in range(5)]
    p1, p2, n1, n2 = s[1] + s[4], s[2] + s[3], s[1] - s[4], s[2] - s[3]
    q1, q2, h1, h2 = d[1] - d[4], d[2] - d[3], d[1] + d[4], d[2] + d[3]
    return [
        (s[0] + p1 + p2, None),
        (d[0] + COS36 * q1 + COS72 * q2, -SIN36 * h1 - SIN72 * h2),
        (s[0] + COS72 * p1 - COS36 * p2, -SIN72 * n1 - SIN36 * n2),
        (d[0] - COS72 * q1 - COS36 * q2, SIN36 * h2 - SIN72 * h1),
        (s[0] - COS36 * p1 + COS72 * p2, SIN72 * n2 - SIN36 * n1),
        (d[0] - q1 + q2, None),
    ]


def grid_kernel(
    in_ref, choice_ref, weight_ref, synth_ref, anal_ref, twiddle_ref, out_ref,
    coeff, spread, fields, back
):
    columns = jnp.concatenate(
        [in_ref[pl.ds(0, SLOTS, stride=2), :].T, in_ref[pl.ds(1, SLOTS, stride=2), :].T[:32]], axis=0
    )
    choice = choice_ref[...]
    picked = jnp.dot(
        jnp.concatenate(split(columns), axis=0), choice, preferred_element_type=F32
    )
    lane = lax.broadcasted_iota(jnp.int32, (8, 128), 1)
    left = lane < FINE
    first_wave = (lane & (FINE - 1)) < FINE // 2
    mean_scale = jnp.where((lane & (FINE - 1)) == 0, 0.5, 1.0)
    for level in range(2):
        for i in range(HALF_ROWS):
            for q in range(RADIX // 2):
                base, cols = level * 160 + i * 32, slice(q * 128, q * 128 + 128)
                real = jnp.where(
                    first_wave, picked[base : base + 8, cols], picked[base + 16 : base + 24, cols]
                )
                imag = jnp.where(
                    first_wave, picked[base + 8 : base + 16, cols], picked[base + 24 : base + 32, cols]
                )
                even = jnp.where(left, real, pltpu.roll(imag, 64, 1))
                odd = jnp.where(left, pltpu.roll(real, 64, 1), imag)
                if q == 0:
                    even = even * mean_scale
                at = i * 80 + q * 16
                coeff[at : at + 8, level * 128 : level * 128 + 128] = even
                coeff[at + 8 : at + 16, level * 128 : level * 128 + 128] = odd
    both = coeff[...].astype(BF)
    spread[...] = jnp.dot(
        jnp.concatenate([both, both[:, :128]], axis=1), synth_ref[...], preferred_element_type=F32
    )
    for i in range(HALF_ROWS):
        real, imag = [], []
        for r in range(RADIX):
            at = i * 80 + r * 8
            zr, zi = spread[at : at + 8, :SEG], spread[at : at + 8, SEG:]
            if r == 0:
                real.append(zr)
                imag.append(None)
                continue
            tr, ti = twiddle_ref[r : r + 1, :], twiddle_ref[RADIX + r : RADIX + r + 1, :]
            real.append(tr * zr - ti * zi)
            imag.append(None if r == 5 else tr * zi + ti * zr)
        value = jnp.concatenate(to_segments(real, imag), axis=1)
        moved = weight_ref[i, 0:1, :] * value
        for offset in range(1, REACH + 1):
            moved = moved + weight_ref[i, offset : offset + 1, :] * pltpu.roll(value, offset, 1)
        waves = from_segments([moved[:, k * SEG : k * SEG + SEG] for k in range(RADIX)])
        for r in range(RADIX):
            vr, vi = waves[r] if r < 6 else waves[RADIX - r]
            if r > 5:
                vi = -vi
            at = i * 80 + r * 8
            if r == 0:
                fields[at : at + 8, :SEG] = vr
                fields[at : at + 8, SEG:] = jnp.zeros_like(vr)
                continue
            tr, ti = twiddle_ref[r : r + 1, :], twiddle_ref[RADIX + r : RADIX + r + 1, :]
            if vi is None:
                fields[at : at + 8, :SEG] = tr * vr
                fields[at : at + 8, SEG:] = -ti * vr
            else:
                fields[at : at + 8, :SEG] = tr * vr + ti * vi
                fields[at : at + 8, SEG:] = tr * vi - ti * vr
    wide = jnp.dot(
        jnp.concatenate(split(fields[...]), axis=0), anal_ref[...], preferred_element_type=F32
    )
    result = wide[:400, :128] + wide[:400, 128:] + wide[400:, :128]
    for i in range(HALF_ROWS):
        for q in range(RADIX // 2):
            at, cols = i * 80 + q * 16, slice(q * 128, q * 128 + 128)
            even, odd = result[at : at + 8], result[at + 8 : at + 16]
            real = jnp.where(left, even, pltpu.roll(odd, 64, 1))
            imag = jnp.where(left, pltpu.roll(even, 64, 1), odd)
            base = i * 32
            back[base : base + 8, cols] = jnp.where(first_wave, real, 0.0)
            back[base + 8 : base + 16, cols] = jnp.where(first_wave, imag, 0.0)
            back[base + 16 : base + 24, cols] = jnp.where(first_wave, 0.0, real)
            back[base + 24 : base + 32, cols] = jnp.where(first_wave, 0.0, imag)
    sent = lax.dot_general(
        jnp.concatenate(split(back[...]), axis=0), choice, (((1,), (1,)), ((), ())),
        preferred_element_type=F32,
    )
    sent = sent[:160] + sent[160:]
    out_ref[pl.ds(0, SLOTS, stride=2), :] = sent[:128].T
    out_ref[pl.ds(1, SLOTS, stride=2), 0:32] = sent[128:].T


def analysis_kernel(pairs_ref, in_ref, table_ref, out_ref, turned):
    lane = lax.broadcasted_iota(jnp.int32, (32, 128), 1)
    left = lane < 64
    for g in range(4):
        shared = []
        for f in range(2):
            at = (2 * g + f) * 128
            north, north_last = (in_ref[pl.ds(at + c, 32, stride=2), :] for c in range(2))
            south, south_last = (
                backwards(in_ref[pl.ds(at + 64 + c, 32, stride=2), :]) for c in range(2)
            )
            turned[pl.ds(5 * g + 3 * f, 32, stride=20), :] = jnp.where(
                left, north, pltpu.roll(south, 64, 1)
            )
            turned[pl.ds(5 * g + 3 * f + 1, 32, stride=20), :] = jnp.where(
                left, pltpu.roll(north, 64, 1), south
            )
            shared += [north_last, south_last]
        turned[pl.ds(5 * g + 2, 32, stride=20), :] = jnp.where(
            left,
            jnp.where(lane < 32, shared[0], pltpu.roll(shared[2], 32, 1)),
            jnp.where(lane < 96, pltpu.roll(shared[1], 64, 1), pltpu.roll(shared[3], 96, 1)),
        )
    straight = turned[...].T
    north, south_rows = straight[:64], straight[64:]
    table_high, table_low = split(table_ref[0])
    product = dot3(
        jnp.concatenate([north + south_rows, north - south_rows], axis=0), table_high, table_low
    )
    pair = own_pair(pairs_ref)
    upper, odd = wave_rows(pair)
    live = pair < PAIRS
    even = odd == 0
    for half in range(2):
        for part in range(2):
            rows = [
                [
                    product[
                        parity * 64 + half * 32 + wave * 16 + part * 8 :
                        parity * 64 + half * 32 + wave * 16 + part * 8 + 8
                    ]
                    for parity in range(2)
                ]
                for wave in range(2)
            ]
            value = jnp.where(
                upper,
                jnp.where(even, rows[0][0], rows[0][1]),
                jnp.where(even, rows[1][0], rows[1][1]),
            )
            first = part * 16 + half * 8
            out_ref[0, first : first + 8, :] = jnp.where(live, value, 0.0)


VMEM = pl.BlockSpec(memory_space=pltpu.VMEM)
PARAMS = pltpu.CompilerParams(vmem_limit_bytes=40 * 1024 * 1024)


def slot_choice(slot_pair):
    column = jnp.arange(RADIX * FINE, dtype=jnp.int32)
    wave = (column % FINE) * RADIX + column // FINE
    pair = jnp.where(wave < PAIRS, wave, WAVES - 1 - wave)
    return (slot_pair[:, None] == pair[None, :]).astype(BF)


def advection_weights(cells, fraction, band, lon, bands):
    position = jnp.arange(HALF_ROWS, dtype=jnp.int32)
    position = jnp.where(lon % 2 == 0, position, (position + 1) % HALF_ROWS)
    row = (HALF_ROWS * lon + position) // 2
    row = jnp.where(band < bands // 2, row, cells.shape[0] - 1 - row)
    cells = jnp.take(cells, row, axis=0)[:, None, :]
    fraction = jnp.take(fraction, row, axis=0)[:, None, :]
    offset = jnp.arange(REACH + 1, dtype=jnp.int32)[None, :, None]
    return jnp.where(cells == offset, 1.0 - fraction, 0.0) + jnp.where(
        cells == offset - 1, fraction, 0.0
    )


def legendre_synthesis(slot_pair, spectral_in, leg_synthesis):
    return pl.pallas_call(
        synthesis_kernel,
        out_shape=jax.ShapeDtypeStruct((2 * SLOTS, 128), F32),
        in_specs=[VMEM] * 3,
        out_specs=VMEM,
        scratch_shapes=[
            pltpu.VMEM((HALF, 128), F32),
        ],
        compiler_params=PARAMS,
        name="legendre_synthesis",
    )(slot_pair.reshape(-1, 128), spectral_in, leg_synthesis)


def grid_step(arrived, choice, weights):
    return pl.pallas_call(
        grid_kernel,
        out_shape=jax.ShapeDtypeStruct((2 * SLOTS, 128), F32),
        in_specs=[VMEM] * 6,
        out_specs=VMEM,
        scratch_shapes=[
            pltpu.VMEM((400, 256), F32),
            pltpu.VMEM((400, 2 * SEG), F32),
            pltpu.VMEM((400, 2 * SEG), F32),
            pltpu.VMEM((160, WAVES), F32),
        ],
        compiler_params=PARAMS,
        name="grid_step",
    )(arrived, choice, weights, *fine_tables())


def legendre_analysis(slot_pair, returned, leg_analysis):
    return pl.pallas_call(
        analysis_kernel,
        out_shape=jax.ShapeDtypeStruct((1, 32, ROWS), F32),
        in_specs=[VMEM] * 3,
        out_specs=VMEM,
        scratch_shapes=[pltpu.VMEM((HALF, 128), F32)],
        compiler_params=PARAMS,
        name="legendre_analysis",
    )(slot_pair.reshape(-1, 128), returned, leg_analysis)


def exchange(messages):
    return lax.all_to_all(
        messages.reshape(SLOTS, 2, 128), ("lon", "band"), split_axis=0, concat_axis=0, tiled=True
    ).reshape(2 * SLOTS, 128)


def per_device(
    spectral_in, leg_synthesis, leg_analysis, slot_pair, departure_cells, departure_frac
):
    arrived = exchange(legendre_synthesis(slot_pair, spectral_in, leg_synthesis))
    lons = lax.axis_size("lon")
    choice = slot_choice(slot_pair.reshape(-1, lons).T.reshape(-1))
    weights = advection_weights(
        departure_cells, departure_frac, lax.axis_index("band"), lax.axis_index("lon"),
        lax.axis_size("band"),
    )
    returned = exchange(grid_step(arrived, choice, weights))
    return legendre_analysis(slot_pair, returned, leg_analysis)


def solution(mesh):
    return jax.shard_map(
        per_device,
        mesh=mesh,
        in_specs=(
            P(("band", "lon"), None, None),
            P(("band", "lon"), None, None),
            P(("band", "lon"), None, None),
            P(),
            P("band", None),
            P("band", None),
        ),
        out_specs=P(("band", "lon"), None, None),
        check_vma=False,
    )
```

```python
import math

import jax
import jax.numpy as jnp
import ml_dtypes
import numpy as np
from jax import lax
from jax.experimental import pallas as pl
from jax.experimental.pallas import tpu as pltpu
from jax.sharding import PartitionSpec as P

WAVES = 640
PAIRS = 320
ROWS = 641
HALF = 640
NLON = 2560
SLOTS = 512
RADIX = 10
FINE = 64
SEG = 256
HALF_ROWS = 5
REACH = 4
BF = jnp.bfloat16
F32 = jnp.float32


def halves(table):
    high = table.astype(np.float32).astype(ml_dtypes.bfloat16)
    low = (table - high.astype(np.float64)).astype(np.float32).astype(ml_dtypes.bfloat16)
    return high, low


def fine_tables():
    place = np.arange(SEG)
    phase = 2 * math.pi * ((np.arange(FINE)[:, None] * place[None, :]) % SEG) / SEG
    cos, sin = np.cos(phase), np.sin(phase)
    synth = np.block([[2 * cos, 2 * sin], [-2 * sin, 2 * cos]])
    high, low = halves(synth)
    anal_high, anal_low = halves(synth.T / (2 * NLON))
    turn = 2 * math.pi * ((np.arange(RADIX)[:, None] * place[None, :]) % NLON) / NLON
    twiddle = np.concatenate([np.cos(turn), np.sin(turn)], axis=0).astype(np.float32)
    return (
        np.concatenate([high, high, low], axis=0),
        np.concatenate([anal_high, anal_low], axis=1),
        twiddle,
    )


def split(value):
    high = value.astype(BF)
    return high, (value - high.astype(F32)).astype(BF)


def dot3(left, right_high, right_low):
    high, low = split(left)
    rows = left.shape[0]
    both = jnp.dot(
        jnp.concatenate([high, low], axis=0), right_high, preferred_element_type=F32
    )
    return both[:rows] + both[rows:] + jnp.dot(high, right_low, preferred_element_type=F32)


def wave_rows(pair):
    row = lax.broadcasted_iota(jnp.int32, (1, ROWS), 1)
    cut = WAVES - pair
    upper = row < cut
    odd = jnp.where(upper, row, row - cut) & 1
    return upper, odd


def own_pair(pairs_ref):
    slot = lax.axis_index("band") * lax.axis_size("lon") + lax.axis_index("lon")
    shape = pairs_ref.shape
    index = lax.broadcasted_iota(jnp.int32, shape, 0) * shape[1] + lax.broadcasted_iota(
        jnp.int32, shape, 1
    )
    mine = jnp.where(index == slot, pairs_ref[...], 0)
    return jnp.sum(jnp.sum(mine, axis=1, keepdims=True), axis=0, keepdims=True)


def backwards(value):
    row = lax.broadcasted_iota(jnp.int32, (8, 128), 0)
    parts = [
        jnp.take_along_axis(value[at : at + 8], 7 - row, axis=0, mode="promise_in_bounds")
        for at in range(value.shape[0] - 8, -1, -8)
    ]
    return jnp.concatenate(parts, axis=0)


def leave(built, out_hbm, sent, n):
    rows = pl.ds(n * 256, 256)
    return pltpu.make_async_copy(built.at[rows, :], out_hbm.at[rows, :], sent.at[n])


def synthesis_kernel(pairs_ref, spec_ref, table_ref, out_hbm, turned, out_ref, sent):
    pair = own_pair(pairs_ref)
    upper, odd = wave_rows(pair)
    live = pair < PAIRS
    groups = []
    for parity in range(2):
        for half in range(2):
            for wave in range(2):
                mask = jnp.logical_and(upper if wave == 0 else jnp.logical_not(upper), odd == parity)
                mask = jnp.logical_and(mask, live)
                for part in range(2):
                    first = part * 16 + half * 8
                    groups.append(jnp.where(mask, spec_ref[0, first : first + 8, :], 0.0))
    table_high, table_low = split(table_ref[0])
    product = dot3(jnp.concatenate(groups, axis=0), table_high, table_low)
    even, odd_sum = product[:64], product[64:]
    turned[...] = jnp.concatenate([even + odd_sum, even - odd_sum], axis=0).T
    lane = lax.broadcasted_iota(jnp.int32, (32, 128), 1)
    left = lane < 64
    for g in range(4):
        pick = [turned[pl.ds(5 * g + u, 32, stride=20), :] for u in range(5)]
        rolled = [pltpu.roll(q, 64, 1) for q in pick]
        for f in range(2):
            at = (2 * g + f) * 128
            out_ref[pl.ds(at, 32, stride=2), :] = jnp.where(left, pick[3 * f], rolled[3 * f + 1])
            out_ref[pl.ds(at + 1, 32, stride=2), :] = pltpu.roll(pick[2], 96, 1) if f else pick[2]
            out_ref[pl.ds(at + 64, 32, stride=2), :] = backwards(
                jnp.where(left, rolled[3 * f], pick[3 * f + 1])
            )
            out_ref[pl.ds(at + 65, 32, stride=2), :] = backwards(
                pltpu.roll(pick[2], 32, 1) if f else rolled[2]
            )
        leave(out_ref, out_hbm, sent, g).start()
    for g in range(4):
        leave(out_ref, out_hbm, sent, g).wait()


def circle(degrees):
    return math.cos(math.radians(degrees)), math.sin(math.radians(degrees))


COS36, SIN36 = circle(36)
COS72, SIN72 = circle(72)


def to_segments(real, imag):
    p1, p2 = real[2] + real[8], real[4] + real[6]
    n1, n2 = imag[2] - imag[8], imag[4] - imag[6]
    a1, b1 = real[0] + COS72 * p1 - COS36 * p2, SIN72 * n1 + SIN36 * n2
    a2, b2 = real[0] - COS36 * p1 + COS72 * p2, SIN36 * n1 - SIN72 * n2
    evens = [real[0] + p1 + p2, a1 - b1, a2 - b2, a2 + b2, a1 + b1]
    q1, q3 = real[1] + real[9], real[3] + real[7]
    h1, h3 = imag[1] - imag[9], imag[3] - imag[7]
    a1, b1 = COS36 * q1 - COS72 * q3 - real[5], SIN36 * h1 + SIN72 * h3
    a2, b2 = real[5] + COS72 * q1 - COS36 * q3, SIN72 * h1 - SIN36 * h3
    odds = [real[5] + q1 + q3, a1 - b1, a2 - b2, -a2 - b2, -a1 - b1]
    return [e + o for e, o in zip(evens, odds)] + [e - o for e, o in zip(evens, odds)]


def from_segments(parts):
    s = [parts[k] + parts[k + 5] for k in range(5)]
    d = [parts[k] - parts[k + 5] for k in range(5)]
    p1, p2, n1, n2 = s[1] + s[4], s[2] + s[3], s[1] - s[4], s[2] - s[3]
    q1, q2, h1, h2 = d[1] - d[4], d[2] - d[3], d[1] + d[4], d[2] + d[3]
    return [
        (s[0] + p1 + p2, None),
        (d[0] + COS36 * q1 + COS72 * q2, -SIN36 * h1 - SIN72 * h2),
        (s[0] + COS72 * p1 - COS36 * p2, -SIN72 * n1 - SIN36 * n2),
        (d[0] - COS72 * q1 - COS36 * q2, SIN36 * h2 - SIN72 * h1),
        (s[0] - COS36 * p1 + COS72 * p2, SIN72 * n2 - SIN36 * n1),
        (d[0] - q1 + q2, None),
    ]


def grid_kernel(
    in_ref, choice_ref, weight_ref, synth_ref, anal_ref, twiddle_ref, out_hbm,
    coeff, spread, fields, back, out_ref, left_core
):
    columns = jnp.concatenate(
        [in_ref[pl.ds(0, SLOTS, stride=2), :].T, in_ref[pl.ds(1, SLOTS, stride=2), :].T[:32]], axis=0
    )
    choice = choice_ref[...]
    picked = jnp.dot(
        jnp.concatenate(split(columns), axis=0), choice, preferred_element_type=F32
    )
    lane = lax.broadcasted_iota(jnp.int32, (8, 128), 1)
    left = lane < FINE
    first_wave = (lane & (FINE - 1)) < FINE // 2
    mean_scale = jnp.where((lane & (FINE - 1)) == 0, 0.5, 1.0)
    for level in range(2):
        for i in range(HALF_ROWS):
            for q in range(RADIX // 2):
                base, cols = level * 160 + i * 32, slice(q * 128, q * 128 + 128)
                real = jnp.where(
                    first_wave, picked[base : base + 8, cols], picked[base + 16 : base + 24, cols]
                )
                imag = jnp.where(
                    first_wave, picked[base + 8 : base + 16, cols], picked[base + 24 : base + 32, cols]
                )
                even = jnp.where(left, real, pltpu.roll(imag, 64, 1))
                odd = jnp.where(left, pltpu.roll(real, 64, 1), imag)
                if q == 0:
                    even = even * mean_scale
                at = i * 80 + q * 16
                coeff[at : at + 8, level * 128 : level * 128 + 128] = even
                coeff[at + 8 : at + 16, level * 128 : level * 128 + 128] = odd
    both = coeff[...].astype(BF)
    spread[...] = jnp.dot(
        jnp.concatenate([both, both[:, :128]], axis=1), synth_ref[...], preferred_element_type=F32
    )
    for i in range(HALF_ROWS):
        real, imag = [], []
        for r in range(RADIX):
            at = i * 80 + r * 8
            zr, zi = spread[at : at + 8, :SEG], spread[at : at + 8, SEG:]
            if r == 0:
                real.append(zr)
                imag.append(None)
                continue
            tr, ti = twiddle_ref[r : r + 1, :], twiddle_ref[RADIX + r : RADIX + r + 1, :]
            real.append(tr * zr - ti * zi)
            imag.append(None if r == 5 else tr * zi + ti * zr)
        value = jnp.concatenate(to_segments(real, imag), axis=1)
        behind = pltpu.roll(value, 1, 1)
        w = [weight_ref[i, n : n + 1, :] for n in range(REACH + 1)]
        inner = w[2] * value + w[3] * behind + pltpu.roll(w[4] * value, 2, 1)
        moved = w[0] * value + w[1] * behind + pltpu.roll(inner, 2, 1)
        waves = from_segments([moved[:, k * SEG : k * SEG + SEG] for k in range(RADIX)])
        for r in range(RADIX):
            vr, vi = waves[r] if r < 6 else waves[RADIX - r]
            if r > 5:
                vi = -vi
            at = i * 80 + r * 8
            if r == 0:
                fields[at : at + 8, :SEG] = vr
                fields[at : at + 8, SEG:] = jnp.zeros_like(vr)
                continue
            tr, ti = twiddle_ref[r : r + 1, :], twiddle_ref[RADIX + r : RADIX + r + 1, :]
            if vi is None:
                fields[at : at + 8, :SEG] = tr * vr
                fields[at : at + 8, SEG:] = -ti * vr
            else:
                fields[at : at + 8, :SEG] = tr * vr + ti * vi
                fields[at : at + 8, SEG:] = tr * vi - ti * vr
    wide = jnp.dot(
        jnp.concatenate(split(fields[...]), axis=0), anal_ref[...], preferred_element_type=F32
    )
    result = wide[:400, :128] + wide[:400, 128:] + wide[400:, :128]
    for i in range(HALF_ROWS):
        for q in range(RADIX // 2):
            at, cols = i * 80 + q * 16, slice(q * 128, q * 128 + 128)
            even, odd = result[at : at + 8], result[at + 8 : at + 16]
            real = jnp.where(left, even, pltpu.roll(odd, 64, 1))
            imag = jnp.where(left, pltpu.roll(even, 64, 1), odd)
            base = i * 32
            back[base : base + 8, cols] = jnp.where(first_wave, real, 0.0)
            back[base + 8 : base + 16, cols] = jnp.where(first_wave, imag, 0.0)
            back[base + 16 : base + 24, cols] = jnp.where(first_wave, 0.0, real)
            back[base + 24 : base + 32, cols] = jnp.where(first_wave, 0.0, imag)
    sent = lax.dot_general(
        jnp.concatenate(split(back[...]), axis=0), choice, (((1,), (1,)), ((), ())),
        preferred_element_type=F32,
    )
    sent = sent[:160] + sent[160:]
    for n in range(4):
        block = sent[:, n * 128 : n * 128 + 128]
        out_ref[pl.ds(n * 256, 128, stride=2), :] = block[:128].T
        out_ref[pl.ds(n * 256 + 1, 128, stride=2), 0:32] = block[128:].T
        leave(out_ref, out_hbm, left_core, n).start()
    for n in range(4):
        leave(out_ref, out_hbm, left_core, n).wait()


def analysis_kernel(pairs_ref, in_ref, table_ref, out_ref, turned):
    lane = lax.broadcasted_iota(jnp.int32, (32, 128), 1)
    left = lane < 64
    for g in range(4):
        shared = []
        for f in range(2):
            at = (2 * g + f) * 128
            north, north_last = (in_ref[pl.ds(at + c, 32, stride=2), :] for c in range(2))
            south, south_last = (
                backwards(in_ref[pl.ds(at + 64 + c, 32, stride=2), :]) for c in range(2)
            )
            turned[pl.ds(5 * g + 3 * f, 32, stride=20), :] = jnp.where(
                left, north, pltpu.roll(south, 64, 1)
            )
            turned[pl.ds(5 * g + 3 * f + 1, 32, stride=20), :] = jnp.where(
                left, pltpu.roll(north, 64, 1), south
            )
            shared += [north_last, south_last]
        turned[pl.ds(5 * g + 2, 32, stride=20), :] = jnp.where(
            left,
            jnp.where(lane < 32, shared[0], pltpu.roll(shared[2], 32, 1)),
            jnp.where(lane < 96, pltpu.roll(shared[1], 64, 1), pltpu.roll(shared[3], 96, 1)),
        )
    straight = turned[...].T
    north, south_rows = straight[:64], straight[64:]
    table_high, table_low = split(table_ref[0])
    product = dot3(
        jnp.concatenate([north + south_rows, north - south_rows], axis=0), table_high, table_low
    )
    pair = own_pair(pairs_ref)
    upper, odd = wave_rows(pair)
    live = pair < PAIRS
    even = odd == 0
    for half in range(2):
        for part in range(2):
            rows = [
                [
                    product[
                        parity * 64 + half * 32 + wave * 16 + part * 8 :
                        parity * 64 + half * 32 + wave * 16 + part * 8 + 8
                    ]
                    for parity in range(2)
                ]
                for wave in range(2)
            ]
            value = jnp.where(
                upper,
                jnp.where(even, rows[0][0], rows[0][1]),
                jnp.where(even, rows[1][0], rows[1][1]),
            )
            first = part * 16 + half * 8
            out_ref[0, first : first + 8, :] = jnp.where(live, value, 0.0)


VMEM = pl.BlockSpec(memory_space=pltpu.VMEM)
HBM = pl.BlockSpec(memory_space=pltpu.HBM)
PARAMS = pltpu.CompilerParams(vmem_limit_bytes=40 * 1024 * 1024)


def slot_choice(slot_pair):
    column = jnp.arange(RADIX * FINE, dtype=jnp.int32)
    wave = (column % FINE) * RADIX + column // FINE
    pair = jnp.where(wave < PAIRS, wave, WAVES - 1 - wave)
    return (slot_pair[:, None] == pair[None, :]).astype(BF)


def advection_weights(cells, fraction, band, lon, bands):
    position = jnp.arange(HALF_ROWS, dtype=jnp.int32)
    position = jnp.where(lon % 2 == 0, position, (position + 1) % HALF_ROWS)
    row = (HALF_ROWS * lon + position) // 2
    row = jnp.where(band < bands // 2, row, cells.shape[0] - 1 - row)
    cells = jnp.take(cells, row, axis=0)[:, None, :]
    fraction = jnp.take(fraction, row, axis=0)[:, None, :]
    offset = jnp.arange(REACH + 1, dtype=jnp.int32)[None, :, None]
    weight = jnp.where(cells == offset, 1.0 - fraction, 0.0) + jnp.where(
        cells == offset - 1, fraction, 0.0
    )
    return jnp.concatenate(
        [weight[:, :2], jnp.roll(weight[:, 2:4], -2, axis=2), jnp.roll(weight[:, 4:], -4, axis=2)],
        axis=1,
    )


def legendre_synthesis(slot_pair, spectral_in, leg_synthesis):
    return pl.pallas_call(
        synthesis_kernel,
        out_shape=jax.ShapeDtypeStruct((2 * SLOTS, 128), F32),
        in_specs=[VMEM] * 3,
        out_specs=HBM,
        scratch_shapes=[
            pltpu.VMEM((HALF, 128), F32),
            pltpu.VMEM((2 * SLOTS, 128), F32),
            pltpu.SemaphoreType.DMA((4,)),
        ],
        compiler_params=PARAMS,
        name="legendre_synthesis",
    )(slot_pair.reshape(-1, 128), spectral_in, leg_synthesis)


def grid_step(arrived, choice, weights):
    return pl.pallas_call(
        grid_kernel,
        out_shape=jax.ShapeDtypeStruct((2 * SLOTS, 128), F32),
        in_specs=[VMEM] * 6,
        out_specs=HBM,
        scratch_shapes=[
            pltpu.VMEM((400, 256), F32),
            pltpu.VMEM((400, 2 * SEG), F32),
            pltpu.VMEM((400, 2 * SEG), F32),
            pltpu.VMEM((160, WAVES), F32),
            pltpu.VMEM((2 * SLOTS, 128), F32),
            pltpu.SemaphoreType.DMA((4,)),
        ],
        compiler_params=PARAMS,
        name="grid_step",
    )(arrived, choice, weights, *fine_tables())


def legendre_analysis(slot_pair, returned, leg_analysis):
    return pl.pallas_call(
        analysis_kernel,
        out_shape=jax.ShapeDtypeStruct((1, 32, ROWS), F32),
        in_specs=[VMEM] * 3,
        out_specs=VMEM,
        scratch_shapes=[pltpu.VMEM((HALF, 128), F32)],
        compiler_params=PARAMS,
        name="legendre_analysis",
    )(slot_pair.reshape(-1, 128), returned, leg_analysis)


def exchange(messages):
    return lax.all_to_all(
        messages.reshape(SLOTS, 2, 128), ("lon", "band"), split_axis=0, concat_axis=0, tiled=True
    ).reshape(2 * SLOTS, 128)


def per_device(
    spectral_in, leg_synthesis, leg_analysis, slot_pair, departure_cells, departure_frac
):
    arrived = exchange(legendre_synthesis(slot_pair, spectral_in, leg_synthesis))
    lons = lax.axis_size("lon")
    choice = slot_choice(slot_pair.reshape(-1, lons).T.reshape(-1))
    weights = advection_weights(
        departure_cells, departure_frac, lax.axis_index("band"), lax.axis_index("lon"),
        lax.axis_size("band"),
    )
    returned = exchange(grid_step(arrived, choice, weights))
    return legendre_analysis(slot_pair, returned, leg_analysis)


def solution(mesh):
    return jax.shard_map(
        per_device,
        mesh=mesh,
        in_specs=(
            P(("band", "lon"), None, None),
            P(("band", "lon"), None, None),
            P(("band", "lon"), None, None),
            P(),
            P("band", None),
            P("band", None),
        ),
        out_specs=P(("band", "lon"), None, None),
        check_vma=False,
    )
```

```python
import math

import jax
import jax.numpy as jnp
import ml_dtypes
import numpy as np
from jax import lax
from jax.experimental import pallas as pl
from jax.experimental.pallas import tpu as pltpu
from jax.sharding import PartitionSpec as P

WAVES = 640
PAIRS = 320
ROWS = 641
HALF = 640
NLON = 2560
SLOTS = 512
RADIX = 10
FINE = 64
SEG = 256
HALF_ROWS = 5
REACH = 4
BF = jnp.bfloat16
F32 = jnp.float32


def halves(table):
    high = table.astype(np.float32).astype(ml_dtypes.bfloat16)
    low = (table - high.astype(np.float64)).astype(np.float32).astype(ml_dtypes.bfloat16)
    return high, low


def fine_tables():
    place = np.arange(SEG)
    phase = 2 * math.pi * ((np.arange(FINE)[:, None] * place[None, :]) % SEG) / SEG
    cos, sin = np.cos(phase), np.sin(phase)
    synth = np.block([[2 * cos, 2 * sin], [-2 * sin, 2 * cos]])
    high, low = halves(synth)
    anal_high, anal_low = halves(synth.T / (2 * NLON))
    turn = 2 * math.pi * ((np.arange(RADIX)[:, None] * place[None, :]) % NLON) / NLON
    twiddle = np.concatenate([np.cos(turn), np.sin(turn)], axis=0).astype(np.float32)
    return (
        np.concatenate([high, high, low], axis=0),
        np.concatenate([anal_high, anal_low], axis=1),
        twiddle,
    )


def split(value):
    high = value.astype(BF)
    return high, (value - high.astype(F32)).astype(BF)


def dot3(left, right_high, right_low):
    high, low = split(left)
    rows = left.shape[0]
    both = jnp.dot(
        jnp.concatenate([high, low], axis=0), right_high, preferred_element_type=F32
    )
    return both[:rows] + both[rows:] + jnp.dot(high, right_low, preferred_element_type=F32)


def wave_rows(pair):
    row = lax.broadcasted_iota(jnp.int32, (1, ROWS), 1)
    cut = WAVES - pair
    upper = row < cut
    odd = jnp.where(upper, row, row - cut) & 1
    return upper, odd


def own_pair(pairs_ref):
    slot = lax.axis_index("band") * lax.axis_size("lon") + lax.axis_index("lon")
    shape = pairs_ref.shape
    index = lax.broadcasted_iota(jnp.int32, shape, 0) * shape[1] + lax.broadcasted_iota(
        jnp.int32, shape, 1
    )
    mine = jnp.where(index == slot, pairs_ref[...], 0)
    return jnp.sum(jnp.sum(mine, axis=1, keepdims=True), axis=0, keepdims=True)


def backwards(value):
    row = lax.broadcasted_iota(jnp.int32, (8, 128), 0)
    parts = [
        jnp.take_along_axis(value[at : at + 8], 7 - row, axis=0, mode="promise_in_bounds")
        for at in range(value.shape[0] - 8, -1, -8)
    ]
    return jnp.concatenate(parts, axis=0)


def leave(built, out_hbm, sent, n):
    rows = pl.ds(n * 256, 256)
    return pltpu.make_async_copy(built.at[rows, :], out_hbm.at[rows, :], sent.at[n])


CUTS = ((0, 384), (384, ROWS - 384))
LANES = HALF // 128


def synthesis_kernel(
    pairs_hbm, spec_hbm, table_hbm, out_hbm, pairs_ref, spec_ref, table, turned, out_ref, arrived, sent
):
    small = [
        pltpu.make_async_copy(pairs_hbm, pairs_ref, arrived.at[0]),
        pltpu.make_async_copy(spec_hbm, spec_ref, arrived.at[1]),
    ]
    large = [
        pltpu.make_async_copy(
            table_hbm.at[pl.ds(LANES * first, LANES * rows), 0, :],
            table.at[pl.ds(LANES * first, LANES * rows), :],
            arrived.at[2 + n],
        )
        for n, (first, rows) in enumerate(CUTS)
    ]
    for copy in large[:1] + small + large[1:]:
        copy.start()
    for copy in small:
        copy.wait()
    pair = own_pair(pairs_ref)
    upper, odd = wave_rows(pair)
    live = pair < PAIRS
    groups = []
    for parity in range(2):
        for half in range(2):
            for wave in range(2):
                mask = jnp.logical_and(upper if wave == 0 else jnp.logical_not(upper), odd == parity)
                mask = jnp.logical_and(mask, live)
                for part in range(2):
                    first = part * 16 + half * 8
                    groups.append(jnp.where(mask, spec_ref[0, first : first + 8, :], 0.0))
    masked = jnp.concatenate(groups, axis=0)
    product = jnp.zeros((128, HALF), F32)
    for copy, (first, rows) in zip(large, CUTS):
        copy.wait()
        block = jnp.concatenate(
            [table[pl.ds(LANES * first + n, rows, stride=LANES), :] for n in range(LANES)], axis=1
        )
        product = product + dot3(masked[:, first : first + rows], *split(block))
    even, odd_sum = product[:64], product[64:]
    turned[...] = jnp.concatenate([even + odd_sum, even - odd_sum], axis=0).T
    lane = lax.broadcasted_iota(jnp.int32, (32, 128), 1)
    left = lane < 64
    for g in range(4):
        pick = [turned[pl.ds(5 * g + u, 32, stride=20), :] for u in range(5)]
        rolled = [pltpu.roll(q, 64, 1) for q in pick]
        for f in range(2):
            at = (2 * g + f) * 128
            out_ref[pl.ds(at, 32, stride=2), :] = jnp.where(left, pick[3 * f], rolled[3 * f + 1])
            out_ref[pl.ds(at + 1, 32, stride=2), :] = pltpu.roll(pick[2], 96, 1) if f else pick[2]
            out_ref[pl.ds(at + 64, 32, stride=2), :] = backwards(
                jnp.where(left, rolled[3 * f], pick[3 * f + 1])
            )
            out_ref[pl.ds(at + 65, 32, stride=2), :] = backwards(
                pltpu.roll(pick[2], 32, 1) if f else rolled[2]
            )
        leave(out_ref, out_hbm, sent, g).start()
    for g in range(4):
        leave(out_ref, out_hbm, sent, g).wait()


def circle(degrees):
    return math.cos(math.radians(degrees)), math.sin(math.radians(degrees))


COS36, SIN36 = circle(36)
COS72, SIN72 = circle(72)


def to_segments(real, imag):
    p1, p2 = real[2] + real[8], real[4] + real[6]
    n1, n2 = imag[2] - imag[8], imag[4] - imag[6]
    a1, b1 = real[0] + COS72 * p1 - COS36 * p2, SIN72 * n1 + SIN36 * n2
    a2, b2 = real[0] - COS36 * p1 + COS72 * p2, SIN36 * n1 - SIN72 * n2
    evens = [real[0] + p1 + p2, a1 - b1, a2 - b2, a2 + b2, a1 + b1]
    q1, q3 = real[1] + real[9], real[3] + real[7]
    h1, h3 = imag[1] - imag[9], imag[3] - imag[7]
    a1, b1 = COS36 * q1 - COS72 * q3 - real[5], SIN36 * h1 + SIN72 * h3
    a2, b2 = real[5] + COS72 * q1 - COS36 * q3, SIN72 * h1 - SIN36 * h3
    odds = [real[5] + q1 + q3, a1 - b1, a2 - b2, -a2 - b2, -a1 - b1]
    return [e + o for e, o in zip(evens, odds)] + [e - o for e, o in zip(evens, odds)]


def from_segments(parts):
    s = [parts[k] + parts[k + 5] for k in range(5)]
    d = [parts[k] - parts[k + 5] for k in range(5)]
    p1, p2, n1, n2 = s[1] + s[4], s[2] + s[3], s[1] - s[4], s[2] - s[3]
    q1, q2, h1, h2 = d[1] - d[4], d[2] - d[3], d[1] + d[4], d[2] + d[3]
    return [
        (s[0] + p1 + p2, None),
        (d[0] + COS36 * q1 + COS72 * q2, -SIN36 * h1 - SIN72 * h2),
        (s[0] + COS72 * p1 - COS36 * p2, -SIN72 * n1 - SIN36 * n2),
        (d[0] - COS72 * q1 - COS36 * q2, SIN36 * h2 - SIN72 * h1),
        (s[0] - COS36 * p1 + COS72 * p2, SIN72 * n2 - SIN36 * n1),
        (d[0] - q1 + q2, None),
    ]


def grid_kernel(
    in_ref, choice_ref, weight_ref, synth_ref, anal_ref, twiddle_ref, out_hbm,
    coeff, spread, fields, back, out_ref, left_core
):
    columns = jnp.concatenate(
        [in_ref[pl.ds(0, SLOTS, stride=2), :].T, in_ref[pl.ds(1, SLOTS, stride=2), :].T[:32]], axis=0
    )
    choice = choice_ref[...]
    picked = jnp.dot(
        jnp.concatenate(split(columns), axis=0), choice, preferred_element_type=F32
    )
    lane = lax.broadcasted_iota(jnp.int32, (8, 128), 1)
    left = lane < FINE
    first_wave = (lane & (FINE - 1)) < FINE // 2
    mean_scale = jnp.where((lane & (FINE - 1)) == 0, 0.5, 1.0)
    for level in range(2):
        for i in range(HALF_ROWS):
            for q in range(RADIX // 2):
                base, cols = level * 160 + i * 32, slice(q * 128, q * 128 + 128)
                real = jnp.where(
                    first_wave, picked[base : base + 8, cols], picked[base + 16 : base + 24, cols]
                )
                imag = jnp.where(
                    first_wave, picked[base + 8 : base + 16, cols], picked[base + 24 : base + 32, cols]
                )
                even = jnp.where(left, real, pltpu.roll(imag, 64, 1))
                odd = jnp.where(left, pltpu.roll(real, 64, 1), imag)
                if q == 0:
                    even = even * mean_scale
                at = i * 80 + q * 16
                coeff[at : at + 8, level * 128 : level * 128 + 128] = even
                coeff[at + 8 : at + 16, level * 128 : level * 128 + 128] = odd
    both = coeff[...].astype(BF)
    spread[...] = jnp.dot(
        jnp.concatenate([both, both[:, :128]], axis=1), synth_ref[...], preferred_element_type=F32
    )
    for i in range(HALF_ROWS):
        real, imag = [], []
        for r in range(RADIX):
            at = i * 80 + r * 8
            zr, zi = spread[at : at + 8, :SEG], spread[at : at + 8, SEG:]
            if r == 0:
                real.append(zr)
                imag.append(None)
                continue
            tr, ti = twiddle_ref[r : r + 1, :], twiddle_ref[RADIX + r : RADIX + r + 1, :]
            real.append(tr * zr - ti * zi)
            imag.append(None if r == 5 else tr * zi + ti * zr)
        value = jnp.concatenate(to_segments(real, imag), axis=1)
        behind = pltpu.roll(value, 1, 1)
        w = [weight_ref[i, n : n + 1, :] for n in range(REACH + 1)]
        inner = w[2] * value + w[3] * behind + pltpu.roll(w[4] * value, 2, 1)
        moved = w[0] * value + w[1] * behind + pltpu.roll(inner, 2, 1)
        waves = from_segments([moved[:, k * SEG : k * SEG + SEG] for k in range(RADIX)])
        for r in range(RADIX):
            vr, vi = waves[r] if r < 6 else waves[RADIX - r]
            if r > 5:
                vi = -vi
            at = i * 80 + r * 8
            if r == 0:
                fields[at : at + 8, :SEG] = vr
                fields[at : at + 8, SEG:] = jnp.zeros_like(vr)
                continue
            tr, ti = twiddle_ref[r : r + 1, :], twiddle_ref[RADIX + r : RADIX + r + 1, :]
            if vi is None:
                fields[at : at + 8, :SEG] = tr * vr
                fields[at : at + 8, SEG:] = -ti * vr
            else:
                fields[at : at + 8, :SEG] = tr * vr + ti * vi
                fields[at : at + 8, SEG:] = tr * vi - ti * vr
    wide = jnp.dot(
        jnp.concatenate(split(fields[...]), axis=0), anal_ref[...], preferred_element_type=F32
    )
    result = wide[:400, :128] + wide[:400, 128:] + wide[400:, :128]
    for i in range(HALF_ROWS):
        for q in range(RADIX // 2):
            at, cols = i * 80 + q * 16, slice(q * 128, q * 128 + 128)
            even, odd = result[at : at + 8], result[at + 8 : at + 16]
            real = jnp.where(left, even, pltpu.roll(odd, 64, 1))
            imag = jnp.where(left, pltpu.roll(even, 64, 1), odd)
            base = i * 32
            back[base : base + 8, cols] = jnp.where(first_wave, real, 0.0)
            back[base + 8 : base + 16, cols] = jnp.where(first_wave, imag, 0.0)
            back[base + 16 : base + 24, cols] = jnp.where(first_wave, 0.0, real)
            back[base + 24 : base + 32, cols] = jnp.where(first_wave, 0.0, imag)
    sent = lax.dot_general(
        jnp.concatenate(split(back[...]), axis=0), choice, (((1,), (1,)), ((), ())),
        preferred_element_type=F32,
    )
    sent = sent[:160] + sent[160:]
    for n in range(4):
        block = sent[:, n * 128 : n * 128 + 128]
        out_ref[pl.ds(n * 256, 128, stride=2), :] = block[:128].T
        out_ref[pl.ds(n * 256 + 1, 128, stride=2), 0:32] = block[128:].T
        leave(out_ref, out_hbm, left_core, n).start()
    for n in range(4):
        leave(out_ref, out_hbm, left_core, n).wait()


def analysis_kernel(pairs_ref, in_ref, table_ref, out_ref, turned):
    lane = lax.broadcasted_iota(jnp.int32, (32, 128), 1)
    left = lane < 64
    for g in range(4):
        shared = []
        for f in range(2):
            at = (2 * g + f) * 128
            north, north_last = (in_ref[pl.ds(at + c, 32, stride=2), :] for c in range(2))
            south, south_last = (
                backwards(in_ref[pl.ds(at + 64 + c, 32, stride=2), :]) for c in range(2)
            )
            turned[pl.ds(5 * g + 3 * f, 32, stride=20), :] = jnp.where(
                left, north, pltpu.roll(south, 64, 1)
            )
            turned[pl.ds(5 * g + 3 * f + 1, 32, stride=20), :] = jnp.where(
                left, pltpu.roll(north, 64, 1), south
            )
            shared += [north_last, south_last]
        turned[pl.ds(5 * g + 2, 32, stride=20), :] = jnp.where(
            left,
            jnp.where(lane < 32, shared[0], pltpu.roll(shared[2], 32, 1)),
            jnp.where(lane < 96, pltpu.roll(shared[1], 64, 1), pltpu.roll(shared[3], 96, 1)),
        )
    straight = turned[...].T
    north, south_rows = straight[:64], straight[64:]
    table_high, table_low = split(table_ref[0])
    product = dot3(
        jnp.concatenate([north + south_rows, north - south_rows], axis=0), table_high, table_low
    )
    pair = own_pair(pairs_ref)
    upper, odd = wave_rows(pair)
    live = pair < PAIRS
    even = odd == 0
    for half in range(2):
        for part in range(2):
            rows = [
                [
                    product[
                        parity * 64 + half * 32 + wave * 16 + part * 8 :
                        parity * 64 + half * 32 + wave * 16 + part * 8 + 8
                    ]
                    for parity in range(2)
                ]
                for wave in range(2)
            ]
            value = jnp.where(
                upper,
                jnp.where(even, rows[0][0], rows[0][1]),
                jnp.where(even, rows[1][0], rows[1][1]),
            )
            first = part * 16 + half * 8
            out_ref[0, first : first + 8, :] = jnp.where(live, value, 0.0)


VMEM = pl.BlockSpec(memory_space=pltpu.VMEM)
HBM = pl.BlockSpec(memory_space=pltpu.HBM)
PARAMS = pltpu.CompilerParams(vmem_limit_bytes=40 * 1024 * 1024)


def slot_choice(slot_pair):
    column = jnp.arange(RADIX * FINE, dtype=jnp.int32)
    wave = (column % FINE) * RADIX + column // FINE
    pair = jnp.where(wave < PAIRS, wave, WAVES - 1 - wave)
    return (slot_pair[:, None] == pair[None, :]).astype(BF)


def advection_weights(cells, fraction, band, lon, bands):
    position = jnp.arange(HALF_ROWS, dtype=jnp.int32)
    position = jnp.where(lon % 2 == 0, position, (position + 1) % HALF_ROWS)
    row = (HALF_ROWS * lon + position) // 2
    row = jnp.where(band < bands // 2, row, cells.shape[0] - 1 - row)
    cells = jnp.take(cells, row, axis=0)[:, None, :]
    fraction = jnp.take(fraction, row, axis=0)[:, None, :]
    offset = jnp.arange(REACH + 1, dtype=jnp.int32)[None, :, None]
    weight = jnp.where(cells == offset, 1.0 - fraction, 0.0) + jnp.where(
        cells == offset - 1, fraction, 0.0
    )
    return jnp.concatenate(
        [weight[:, :2], jnp.roll(weight[:, 2:4], -2, axis=2), jnp.roll(weight[:, 4:], -4, axis=2)],
        axis=1,
    )


def legendre_synthesis(slot_pair, spectral_in, leg_synthesis):
    pairs = slot_pair.reshape(-1, 128)
    return pl.pallas_call(
        synthesis_kernel,
        out_shape=jax.ShapeDtypeStruct((2 * SLOTS, 128), F32),
        in_specs=[HBM] * 3,
        out_specs=HBM,
        scratch_shapes=[
            pltpu.VMEM(pairs.shape, jnp.int32),
            pltpu.VMEM(spectral_in.shape, F32),
            pltpu.VMEM((3208, 128), F32),
            pltpu.VMEM((HALF, 128), F32),
            pltpu.VMEM((2 * SLOTS, 128), F32),
            pltpu.SemaphoreType.DMA((2 + len(CUTS),)),
            pltpu.SemaphoreType.DMA((4,)),
        ],
        compiler_params=pltpu.CompilerParams(vmem_limit_bytes=60 * 1024 * 1024),
        name="legendre_synthesis",
    )(pairs, spectral_in, leg_synthesis.reshape(ROWS * LANES, 1, 128))


def grid_step(arrived, choice, weights):
    return pl.pallas_call(
        grid_kernel,
        out_shape=jax.ShapeDtypeStruct((2 * SLOTS, 128), F32),
        in_specs=[VMEM] * 6,
        out_specs=HBM,
        scratch_shapes=[
            pltpu.VMEM((400, 256), F32),
            pltpu.VMEM((400, 2 * SEG), F32),
            pltpu.VMEM((400, 2 * SEG), F32),
            pltpu.VMEM((160, WAVES), F32),
            pltpu.VMEM((2 * SLOTS, 128), F32),
            pltpu.SemaphoreType.DMA((4,)),
        ],
        compiler_params=PARAMS,
        name="grid_step",
    )(arrived, choice, weights, *fine_tables())


def legendre_analysis(slot_pair, returned, leg_analysis):
    return pl.pallas_call(
        analysis_kernel,
        out_shape=jax.ShapeDtypeStruct((1, 32, ROWS), F32),
        in_specs=[VMEM] * 3,
        out_specs=VMEM,
        scratch_shapes=[pltpu.VMEM((HALF, 128), F32)],
        compiler_params=PARAMS,
        name="legendre_analysis",
    )(slot_pair.reshape(-1, 128), returned, leg_analysis)


def exchange(messages):
    return lax.all_to_all(
        messages.reshape(SLOTS, 2, 128), ("lon", "band"), split_axis=0, concat_axis=0, tiled=True
    ).reshape(2 * SLOTS, 128)


def per_device(
    spectral_in, leg_synthesis, leg_analysis, slot_pair, departure_cells, departure_frac
):
    arrived = exchange(legendre_synthesis(slot_pair, spectral_in, leg_synthesis))
    lons = lax.axis_size("lon")
    choice = slot_choice(slot_pair.reshape(-1, lons).T.reshape(-1))
    weights = advection_weights(
        departure_cells, departure_frac, lax.axis_index("band"), lax.axis_index("lon"),
        lax.axis_size("band"),
    )
    returned = exchange(grid_step(arrived, choice, weights))
    return legendre_analysis(slot_pair, returned, leg_analysis)


def solution(mesh):
    return jax.shard_map(
        per_device,
        mesh=mesh,
        in_specs=(
            P(("band", "lon"), None, None),
            P(("band", "lon"), None, None),
            P(("band", "lon"), None, None),
            P(),
            P("band", None),
            P("band", None),
        ),
        out_specs=P(("band", "lon"), None, None),
        check_vma=False,
    )
```
